32 devices in a mesh: replica: 4 (over y, x), shard: 2 (over core), ctx: 4 (over z).
Axes of the slice: x: 2, y: 2, z: 4, core: 2. Of those that a mesh axis runs over, the one named last changes fastest.
Arguments:
- tokens: bfloat16 [16, 1024, 768], P(('replica', 'shard'), 'ctx'), may hold values from -6 to 6
- query_key_value_weight: bfloat16 [768, 2304], P(('shard', 'ctx')), may hold values from -0.21875 to 0.21875
- attention_output_weight: bfloat16 [768, 768], P(('shard', 'ctx')), may hold values from -1.75 to 1.75
- expansion_matrix: bfloat16 [768, 3072], P(('shard', 'ctx')), may hold values from -0.21875 to 0.21875
- feedforward_output_weight: bfloat16 [3072, 768], P(('shard', 'ctx')), may hold values from -0.109375 to 0.109375
- norm_gains: bfloat16 [2, 768], P(None, ('shard', 'ctx')), may hold values from 0.099609375 to 1.8984375
- norm_biases: bfloat16 [2, 768], P(None, ('shard', 'ctx')), may hold values from -3 to 3
- projection_bias_set: bfloat16 [4, 768], P(None, ('shard', 'ctx')), may hold values from -3 to 3
- expansion_offset_vector: bfloat16 [3072], P(('shard', 'ctx')), may hold values from -3 to 3
- cotangent: bfloat16 [16, 1024, 768], P(('replica', 'shard'), 'ctx'), may hold values from -6 to 6
Outputs:
- output: bfloat16 [16, 1024, 768], P(('replica', 'shard'), 'ctx')
- grad_tokens: bfloat16 [16, 1024, 768], P(('replica', 'shard'), 'ctx')
- grad_w_qkv: float32 [768, 2304], P(('shard', 'ctx'))
- grad_w_out: float32 [768, 768], P(('shard', 'ctx'))
- grad_w_in: float32 [768, 3072], P(('shard', 'ctx'))
- grad_w_ffout: float32 [3072, 768], P(('shard', 'ctx'))
- grad_norm_gains: float32 [2, 768], P(None, ('shard', 'ctx'))
- grad_norm_biases: float32 [2, 768], P(None, ('shard', 'ctx'))
- grad_proj_biases: float32 [4, 768], P(None, ('shard', 'ctx'))
- grad_ff_bias: float32 [3072], P(('shard', 'ctx'))
The draws below stay inside these ranges and needn't reach their ends.
All inputs are finite; a program needn't handle non-finite values.
Results may differ from the reference program's by a relative error of at most 0.03.
Values may be sent and summed in bfloat16 or wider, within the bound.
No kernel may reach another device: no remote copies, remote signals or barrier semaphores. Data moves between devices by JAX's collectives and lax.ppermute only.
A program may use at most 256 MiB of HBM per device.

```python
import math
import jax
import jax.numpy as jnp
from jax import lax

D = 768
HEADS = 12
HEAD_DIM = 64
FF = 3072
LEN = 1024
SEQS = 16


def level_of(stream_key, dims, pieces, smallest, largest):
    def one(axis_at, shards_of):
        draws = jax.random.uniform(jax.random.fold_in(jax.random.fold_in(stream_key, 6), axis_at), (shards_of,), jnp.float32, smallest / len(pieces), largest / len(pieces))
        return jnp.repeat(jnp.exp(draws), dims[axis_at] // shards_of).reshape((-1,) + (1,) * (len(dims) - axis_at - 1))

    factor_of = one(*pieces[0])
    for cut in pieces[1:]:
        factor_of = factor_of * one(*cut)
    return factor_of


def noise(stream_key, shape, width, reach, shards=(), held_as=jnp.bfloat16):
    values = jax.random.normal(stream_key, shape, jnp.float32) * width
    if len(shards) > 0:
        values = level_of(stream_key, shape, shards, -0.22, 0.18) * values
    return jnp.clip(values, min=-reach, max=reach).astype(held_as)


def setup_inputs(seed: int = 0) -> dict:
    key_of = jax.random.split(jax.random.key(seed), 11)
    tokens = noise(key_of[0], (SEQS, LEN, D), 1.0, 6.0, ((0, 8), (1, 4)))
    query_key_value_weight = noise(key_of[1], (D, 3 * D), D ** -0.5, 0.21875, ((0, 8),))
    attention_output_weight = noise(key_of[2], (D, D), (max(1, D // 64)) ** -0.5, 1.75, ((0, 8),))
    expansion_matrix = noise(key_of[3], (D, FF), D ** -0.5, 0.21875, ((0, 8),))
    feedforward_output_weight = noise(key_of[4], (FF, D), FF ** -0.5, 0.109375, ((0, 8),))
    norm_gains = jnp.clip(1.0 + 0.18 * jax.random.normal(key_of[5], (2, D), jnp.float32), 0.099609375, 1.8984375).astype(jnp.bfloat16)
    norm_biases = noise(key_of[6], (2, D), 0.5, 3.0, ((1, 8),))
    projection_bias_set = noise(key_of[7], (4, D), 0.5, 3.0, ((1, 8),))
    expansion_offset_vector = noise(key_of[8], (FF,), 0.5, 3.0, ((0, 8),))
    cotangent = noise(key_of[9], (SEQS, LEN, D), 1.0, 6.0, ((0, 8), (1, 4)))
    return {"tokens": tokens, "query_key_value_weight": query_key_value_weight, "attention_output_weight": attention_output_weight, "expansion_matrix": expansion_matrix, "feedforward_output_weight": feedforward_output_weight, "norm_gains": norm_gains, "norm_biases": norm_biases, "projection_bias_set": projection_bias_set, "expansion_offset_vector": expansion_offset_vector, "cotangent": cotangent}


EPS = 1e-05
NEG = -1e+30
EXACT_ARITHMETIC = lax.Precision.HIGHEST

@jax.custom_vjp
def low(v):
    return lax.optimization_barrier(v.astype(jnp.bfloat16)).astype(jnp.float32)

@jax.custom_vjp
def summed_pullback_rule(v):
    return v

def low_keep(v):
    return (low(v), None)

def low_pass(kept, grad):
    return (grad,)

def back_keep(v):
    return (v, None)

def back_low(kept, grad):
    return (low(grad),)
low.defvjp(low_keep, low_pass)
summed_pullback_rule.defvjp(back_keep, back_low)

def layer_norm(values, gain, shift):
    deviation_from_average = values - lax.optimization_barrier(jnp.mean(values, -1, keepdims=True))
    variance = lax.optimization_barrier(jnp.mean(deviation_from_average * deviation_from_average, -1, keepdims=True))
    return deviation_from_average * lax.rsqrt(variance + EPS) * gain + shift

def one_block(keys_all, values_all, block_pair):
    query_rows, first_row = block_pair
    block_rows = query_rows.shape[0]
    key_pos = jnp.arange(keys_all.shape[0], dtype=jnp.int32)
    query_pos = first_row + jnp.arange(block_rows, dtype=jnp.int32)
    scores = jnp.einsum('qhe,khe->hqk', query_rows, keys_all, precision=EXACT_ARITHMETIC)
    scores = jnp.where(key_pos[None, None, :] <= query_pos[None, :, None], scores, NEG)
    weights = low(jax.nn.softmax(summed_pullback_rule(scores), axis=-1))
    return jnp.einsum('hqk,khe->qhe', weights, values_all, precision=EXACT_ARITHMETIC)

def attend(queries, keys_all, values_all):
    seq_len = queries.shape[0]
    block_rows = min(512, seq_len)
    block_count = seq_len // block_rows
    saved_block = jax.checkpoint(one_block)

    def run_block(block_pair):
        return saved_block(keys_all, values_all, block_pair)
    first_rows = jnp.arange(block_count, dtype=jnp.int32) * block_rows
    blocked = queries.reshape(block_count, block_rows, HEADS, HEAD_DIM)
    mixed_out = lax.map(run_block, (blocked, first_rows))
    return mixed_out.reshape(seq_len, HEADS, HEAD_DIM)

def layer(inputs, query_key_value_weight, attention_output_weight, expansion_matrix, feedforward_output_weight, norm_gains, norm_biases, projection_bias_set, expansion_offset_vector):
    scale = HEAD_DIM ** (-0.5)
    first_input_rows = low(layer_norm(inputs, norm_gains[0], norm_biases[0]))
    output_projected = jnp.einsum('xrz,zc->xrc', first_input_rows, query_key_value_weight, precision=EXACT_ARITHMETIC)
    queries = summed_pullback_rule(low((output_projected[..., :D] + projection_bias_set[0]) * scale))
    keys_all = summed_pullback_rule(low(output_projected[..., D:2 * D]))
    values_all = summed_pullback_rule(low(output_projected[..., 2 * D:] + projection_bias_set[1]))
    shape4 = queries.shape[:2] + (HEADS, HEAD_DIM)
    attention_mixed = jax.vmap(attend)(queries.reshape(shape4), keys_all.reshape(shape4), values_all.reshape(shape4))
    attention_mixed = summed_pullback_rule(low(attention_mixed.reshape(inputs.shape)))
    residual_branch = summed_pullback_rule(jnp.einsum('xrz,zc->xrc', attention_mixed, attention_output_weight, precision=EXACT_ARITHMETIC) + projection_bias_set[2])
    hidden_input_rows = inputs + residual_branch
    latter_operand_lines = low(layer_norm(hidden_input_rows, norm_gains[1], norm_biases[1]))
    expanded_activation = summed_pullback_rule(jnp.einsum('ube,ej->ubj', latter_operand_lines, expansion_matrix, precision=EXACT_ARITHMETIC) + expansion_offset_vector)
    activated_hidden = low(jax.nn.gelu(expanded_activation))
    return hidden_input_rows + jnp.einsum('ham,mu->hau', activated_hidden, feedforward_output_weight, precision=EXACT_ARITHMETIC) + projection_bias_set[3]

def reference(tokens, query_key_value_weight, attention_output_weight, expansion_matrix, feedforward_output_weight, norm_gains, norm_biases, projection_bias_set, expansion_offset_vector, cotangent):
    params = tuple((item.astype(jnp.float32) for item in (query_key_value_weight, attention_output_weight, expansion_matrix, feedforward_output_weight, norm_gains, norm_biases, projection_bias_set, expansion_offset_vector)))
    group_size = math.gcd(SEQS, max(1, 4096 // LEN))
    group_count = SEQS // group_size
    token_groups = tokens.reshape(group_count, group_size, LEN, D)
    grad_groups = cotangent.reshape(group_count, group_size, LEN, D)

    def group_step(running, group_pair):
        token_group, grad_group = group_pair
        result, pullback = jax.vjp(layer, token_group.astype(jnp.float32), *params)
        gradients = pullback(grad_group.astype(jnp.float32))
        running = tuple((held + fresh for held, fresh in zip(running, gradients[1:])))
        return (running, (result.astype(jnp.bfloat16), gradients[0].astype(jnp.bfloat16)))
    start_sums = tuple((jnp.zeros(item.shape, jnp.float32) for item in params))
    sums, (outputs, grad_inputs) = lax.scan(group_step, start_sums, (token_groups, grad_groups))
    return (outputs.reshape(SEQS, LEN, D), grad_inputs.reshape(SEQS, LEN, D), sums[0], sums[1], sums[2], sums[3], sums[4], sums[5], sums[6], sums[7])
```

```python
import functools

import jax
import jax.numpy as jnp
from jax import lax
from jax.experimental import pallas as pl
from jax.experimental.pallas import tpu as pltpu
from jax.sharding import PartitionSpec as P

HEADS = 12
HEAD_DIM = 64
EPS = 1e-05
NEG = -1e30
BLOCK = 256
LINE = ("shard", "ctx")
EVERY = ("replica", "shard", "ctx")
BF = jnp.bfloat16
F32 = jnp.float32


def normalize(values):
    centered = values - jnp.mean(values, -1, keepdims=True)
    spread = lax.rsqrt(jnp.mean(centered * centered, -1, keepdims=True) + EPS)
    return centered * spread, spread


def norm_back(upstream, normed, spread):
    first_mean = jnp.mean(upstream, -1, keepdims=True)
    second_mean = jnp.mean(upstream * normed, -1, keepdims=True)
    return spread * (upstream - first_mean - normed * second_mean)


def dot(a, b):
    return jnp.dot(a, b, preferred_element_type=F32)


def dot_nt(a, b):
    return lax.dot_general(a, b, (((1,), (1,)), ((), ())), preferred_element_type=F32)


def dot_tn(a, b):
    return lax.dot_general(a, b, (((0,), (0,)), ((), ())), preferred_element_type=F32)


def place(rank, block, rows):
    per_rank = rows // BLOCK
    owner, part = block // per_rank, block % per_rank
    return pl.multiple_of((owner ^ rank) * rows + part * BLOCK, BLOCK)


def head_mask(lanes, head):
    lane = lax.broadcasted_iota(jnp.int32, (BLOCK, lanes), 1)
    return (lane >= head * HEAD_DIM) & (lane < (head + 1) * HEAD_DIM)


def diagonal(scores):
    key = lax.broadcasted_iota(jnp.int32, scores.shape, 0)
    query = lax.broadcasted_iota(jnp.int32, scores.shape, 1)
    return jnp.where(key <= query, scores, NEG)


def attend_kernel(rows, rank_ref, qkv_ref, mixed_ref, log_ref, keys, values_t):
    length, lanes = mixed_ref.shape
    rank = rank_ref[0]
    heads = lanes // HEAD_DIM
    for block in range(length // BLOCK):
        at = pl.ds(place(rank, block, rows), BLOCK)
        here = slice(block * BLOCK, (block + 1) * BLOCK)
        keys[here, :] = qkv_ref[at, lanes : 2 * lanes]
        values_t[:, here] = qkv_ref[at, 2 * lanes :].T
    for block in range(length // BLOCK):
        at = pl.ds(place(rank, block, rows), BLOCK)
        start, stop = block * BLOCK, (block + 1) * BLOCK
        query = qkv_ref[at, :lanes]
        parts = []
        for head in range(heads):
            one = slice(head * HEAD_DIM, (head + 1) * HEAD_DIM)
            one_query = jnp.where(head_mask(lanes, head), query, jnp.zeros_like(query))
            near = diagonal(dot_nt(keys[start:stop, :], one_query))
            highest = jnp.max(near, 0, keepdims=True)
            if block:
                far = dot_nt(keys[:start, :], one_query)
                highest = jnp.maximum(highest, jnp.max(far, 0, keepdims=True))
            near = jnp.exp(near - highest)
            total = jnp.sum(near, 0, keepdims=True)
            mixed = dot(values_t[one, start:stop], near.astype(BF))
            if block:
                far = jnp.exp(far - highest)
                total = total + jnp.sum(far, 0, keepdims=True)
                mixed = mixed + dot(values_t[one, :start], far.astype(BF))
            parts.append(mixed / total)
            log_ref[head : head + 1, start:stop] = highest + jnp.log(total)
        mixed_ref[at, :] = jnp.concatenate(parts, 0).T.astype(BF)


def attend_back_kernel(
    rows, rank_ref, qkv_ref, grad_ref, log_ref, out_ref, keys, values, keys_t, key_sum, value_sum
):
    length, lanes = grad_ref.shape
    rank = rank_ref[0]
    heads = lanes // HEAD_DIM
    scale = HEAD_DIM ** (-0.5)
    for block in range(length // BLOCK):
        at = pl.ds(place(rank, block, rows), BLOCK)
        here = slice(block * BLOCK, (block + 1) * BLOCK)
        key = qkv_ref[at, lanes : 2 * lanes]
        keys[here, :] = key
        keys_t[:, here] = key.T
        values[here, :] = qkv_ref[at, 2 * lanes :]
    for block in range(length // BLOCK):
        at = pl.ds(place(rank, block, rows), BLOCK)
        start, stop = block * BLOCK, (block + 1) * BLOCK
        query = qkv_ref[at, :lanes]
        grad = grad_ref[at, :]
        parts = []
        near_key = near_value = far_key = far_value = None
        for head in range(heads):
            one = slice(head * HEAD_DIM, (head + 1) * HEAD_DIM)
            mask = head_mask(lanes, head)
            one_query = jnp.where(mask, query, jnp.zeros_like(query))
            one_grad = jnp.where(mask, grad, jnp.zeros_like(grad))
            logs = log_ref[head : head + 1, start:stop]
            near = jnp.exp(diagonal(dot_nt(keys[start:stop, :], one_query)) - logs)
            near_grad = dot_nt(values[start:stop, :], one_grad)
            level = jnp.sum(near * near_grad, 0, keepdims=True)
            if block:
                far = jnp.exp(dot_nt(keys[:start, :], one_query) - logs)
                far_grad = dot_nt(values[:start, :], one_grad)
                level = level + jnp.sum(far * far_grad, 0, keepdims=True)
            near_low = near.astype(BF)
            near_scores = (near * (near_grad - level)).astype(BF)
            value_term, key_term = dot(near_low, one_grad), dot(near_scores, one_query)
            near_value = value_term if near_value is None else near_value + value_term
            near_key = key_term if near_key is None else near_key + key_term
            query_term = dot(keys_t[one, start:stop], near_scores)
            if block:
                far_low = far.astype(BF)
                far_scores = (far * (far_grad - level)).astype(BF)
                value_term, key_term = dot(far_low, one_grad), dot(far_scores, one_query)
                far_value = value_term if far_value is None else far_value + value_term
                far_key = key_term if far_key is None else far_key + key_term
                query_term = query_term + dot(keys_t[one, :start], far_scores)
            parts.append(query_term)
        key_sum[start:stop, :] = near_key
        value_sum[start:stop, :] = near_value
        if block:
            key_sum[:start, :] += far_key
            value_sum[:start, :] += far_value
        query_grad = jnp.concatenate(parts, 0).T.astype(BF).astype(F32) * scale
        out_ref[at, :lanes] = query_grad.astype(BF)
    for block in range(length // BLOCK):
        at = pl.ds(place(rank, block, rows), BLOCK)
        here = slice(block * BLOCK, (block + 1) * BLOCK)
        out_ref[at, lanes : 2 * lanes] = key_sum[here, :].astype(BF)
        out_ref[at, 2 * lanes :] = value_sum[here, :].astype(BF)


def attention_calls(length, rows, groups, lanes):
    heads = lanes // HEAD_DIM
    wide = pl.BlockSpec((length, 3 * lanes), lambda g, r: (0, g))
    thin = pl.BlockSpec((length, lanes), lambda g, r: (0, g))
    logs = pl.BlockSpec((None, heads, length), lambda g, r: (g, 0, 0))
    pairs = groups * heads * length * length // 2
    params = pltpu.CompilerParams(vmem_limit_bytes=56 * 2**20)
    forward = pl.pallas_call(
        functools.partial(attend_kernel, rows),
        grid_spec=pltpu.PrefetchScalarGridSpec(
            num_scalar_prefetch=1,
            grid=(groups,),
            in_specs=[wide],
            out_specs=[thin, logs],
            scratch_shapes=[pltpu.VMEM((length, lanes), BF), pltpu.VMEM((lanes, length), BF)],
        ),
        out_shape=[
            jax.ShapeDtypeStruct((length, groups * lanes), BF),
            jax.ShapeDtypeStruct((groups, heads, length), F32),
        ],
        cost_estimate=pl.CostEstimate(
            flops=pairs * 16 * HEAD_DIM, bytes_accessed=length * groups * lanes * 8, transcendentals=pairs
        ),
        compiler_params=params,
        name="attend",
    )
    backward = pl.pallas_call(
        functools.partial(attend_back_kernel, rows),
        grid_spec=pltpu.PrefetchScalarGridSpec(
            num_scalar_prefetch=1,
            grid=(groups,),
            in_specs=[wide, thin, logs],
            out_specs=wide,
            scratch_shapes=[
                pltpu.VMEM((length, lanes), BF),
                pltpu.VMEM((length, lanes), BF),
                pltpu.VMEM((lanes, length), BF),
                pltpu.VMEM((length, lanes), F32),
                pltpu.VMEM((length, lanes), F32),
            ],
        ),
        out_shape=jax.ShapeDtypeStruct((length, 3 * groups * lanes), BF),
        cost_estimate=pl.CostEstimate(
            flops=pairs * 40 * HEAD_DIM, bytes_accessed=length * groups * lanes * 14, transcendentals=pairs
        ),
        compiler_params=params,
        name="attend_back",
    )
    return forward, backward


def row_moves(shards, spans, seqs):
    chips = spans // (2 * seqs)
    moves = ([], [])
    for shard in range(shards):
        for span in range(spans):
            for item in range(seqs):
                sequence = (shard % 2) * seqs + item
                rank = span // seqs
                target = (shard - shard % 2 + rank % 2) * spans + sequence * chips + rank // 2
                moves[(item + span) % 2].append((shard * spans + span, target))
    return moves


def back_moves(moves):
    return tuple([(b, a) for a, b in one] for one in moves)


def group_moves(shards, spans, ranks):
    chips = ranks // 2
    moves = []
    for k in range(1, ranks):
        one = []
        for shard in range(shards):
            for span in range(spans):
                rank = (span % chips) * 2 + shard % 2
                other = rank ^ k
                target = (shard - shard % 2 + other % 2) * spans + span - span % chips + other // 2
                one.append((shard * spans + span, target))
        moves.append(one)
    return moves


def body(
    tokens, weight_qkv, weight_out, weight_in, weight_back, gains_in, shifts_in, biases_in, ff_bias_in, cotangent
):
    seqs, span, width = tokens.shape
    shards, spans = lax.axis_size("shard"), lax.axis_size("ctx")
    shard, ctx = lax.axis_index("shard"), lax.axis_index("ctx")
    ranks = spans // seqs
    rows, length = seqs * span, spans * span
    chips = ranks // 2
    rank = (ctx % chips) * 2 + shard % 2
    core = shard % 2
    hidden = weight_back.shape[0] * shards * spans
    part, ff_part = width // ranks, hidden // ranks
    blocks = shards * spans
    heads = HEADS // ranks
    lanes = 2 * HEAD_DIM if heads % 2 == 0 else heads * HEAD_DIM
    groups = part // lanes
    scale = HEAD_DIM ** (-0.5)
    moves = row_moves(shards, spans, seqs)
    returns = back_moves(moves)
    turns = group_moves(shards, spans, ranks)
    odd_span = ctx % 2
    odd_sequence = (ctx // chips) % 2
    paired = shards == 2

    def to_rows(items):
        one = lax.ppermute(lax.dynamic_index_in_dim(items, odd_span, 0, False), LINE, moves[0])
        two = lax.ppermute(lax.dynamic_index_in_dim(items, 1 - odd_span, 0, False), LINE, moves[1])
        return jnp.where(odd_sequence == 0, jnp.concatenate([one, two]), jnp.concatenate([two, one]))

    def from_rows(low):
        items = low.reshape(seqs, span, width)
        one = lax.ppermute(lax.dynamic_index_in_dim(items, odd_sequence, 0, False), LINE, returns[0])
        two = lax.ppermute(lax.dynamic_index_in_dim(items, 1 - odd_sequence, 0, False), LINE, returns[1])
        return jnp.where(odd_span == 0, jnp.stack([one, two]), jnp.stack([two, one]))

    def gather_rows(low):
        return jnp.concatenate([low] + [lax.ppermute(low, LINE, one) for one in turns])

    def scatter_rows(partial):
        total = partial[:rows]
        for k, one in enumerate(turns):
            sent = partial[(k + 1) * rows : (k + 2) * rows].astype(BF)
            total = total + lax.ppermute(sent, LINE, one).astype(F32)
        return total

    def swap(items):
        return lax.ppermute(items, "shard", [(0, 1), (1, 0)])

    def gather_columns(weight):
        if not paired:
            whole = lax.all_gather(weight, LINE, axis=0, tiled=True)
            return lax.dynamic_index_in_dim(whole, rank, 1, False)
        mine = lax.dynamic_index_in_dim(weight, core, 1, False)
        other = swap(lax.dynamic_index_in_dim(weight, 1 - core, 1, False))
        both = jnp.where(core == 0, jnp.stack([mine, other]), jnp.stack([other, mine]))
        whole = lax.all_gather(both, "ctx", axis=1)
        return whole.reshape(blocks * weight.shape[0], weight.shape[2])

    def gather_lines(weight):
        if not paired:
            whole = lax.all_gather(weight, LINE, axis=0, tiled=True)
            size = whole.shape[0] // ranks
            return lax.dynamic_slice_in_dim(whole, rank * size, size, 0)
        return lax.all_gather(weight, "ctx", axis=0, tiled=True)

    def scatter_columns(grad):
        low = grad.astype(BF)
        if not paired:
            whole = jnp.zeros((grad.shape[0], ranks, grad.shape[1]), BF)
            whole = lax.dynamic_update_slice_in_dim(whole, low[:, None], rank, 1)
            owned = lax.psum_scatter(whole, LINE, scatter_dimension=0, tiled=True)
            return lax.psum(owned, "replica").astype(F32)
        both = low.reshape(2, spans, -1, grad.shape[1]).swapaxes(0, 1)
        owned = lax.psum_scatter(both, "ctx", scatter_dimension=0, tiled=True)[0]
        owned = lax.psum(owned, "replica")
        mine = lax.dynamic_index_in_dim(owned, core, 0, False)
        other = swap(lax.dynamic_index_in_dim(owned, 1 - core, 0, False))
        mine, other = mine.astype(F32), other.astype(F32)
        return jnp.where(core == 0, jnp.stack([mine, other], 1), jnp.stack([other, mine], 1))

    def scatter_lines(grad):
        low = grad.astype(BF)
        if not paired:
            whole = jnp.zeros((grad.shape[0] * ranks, grad.shape[1]), BF)
            whole = lax.dynamic_update_slice_in_dim(whole, low, rank * grad.shape[0], 0)
            owned = lax.psum_scatter(whole, LINE, scatter_dimension=0, tiled=True)
        else:
            owned = lax.psum_scatter(low, "ctx", scatter_dimension=0, tiled=True)
        return lax.psum(owned, "replica").astype(F32)

    small_in = jnp.concatenate(
        [gains_in, shifts_in, biases_in, ff_bias_in.reshape(hidden // width, width // blocks)]
    )
    small = lax.all_gather(small_in, LINE, axis=0).astype(F32)
    vectors = small[:, :8].swapaxes(0, 1).reshape(8, width)
    gains, shifts, biases = vectors[0:2], vectors[2:4], vectors[4:8]
    ff_bias = lax.dynamic_slice_in_dim(small[:, 8:].reshape(hidden), rank * ff_part, ff_part, 0)

    local = weight_qkv.shape[0]
    ordered = weight_qkv.reshape(local, 3, ranks, groups, lanes).transpose(0, 2, 3, 1, 4)
    qkv_part = gather_columns(ordered.reshape(local, ranks, 3 * part))
    out_part = gather_lines(weight_out)
    in_part = gather_columns(weight_in.reshape(local, ranks, ff_part))
    back_part = gather_lines(weight_back)

    def of_rank(vector):
        return lax.dynamic_slice_in_dim(vector, rank * part, part, 0).reshape(groups, lanes)

    none = jnp.zeros((groups, lanes), F32)
    qkv_bias = jnp.stack([of_rank(biases[0]), none, of_rank(biases[1])], 1).reshape(-1)
    qkv_scale = jnp.stack([none + scale, none + 1, none + 1], 1).reshape(-1)
    attend, attend_back = attention_calls(length, rows, groups, lanes)
    rank_word = rank.astype(jnp.int32).reshape(1)

    inputs = to_rows(tokens).astype(F32)
    grad_low = to_rows(cotangent)
    normed_one, spread_one = normalize(inputs)
    first_all = gather_rows((normed_one * gains[0] + shifts[0]).astype(BF))
    qkv = ((dot(first_all, qkv_part) + qkv_bias) * qkv_scale).astype(BF)
    mixed, logs = attend(rank_word, qkv)
    hidden_in = inputs + scatter_rows(dot(mixed, out_part)) + biases[2]
    normed_two, spread_two = normalize(hidden_in)
    second_all = gather_rows((normed_two * gains[1] + shifts[1]).astype(BF))
    inner = dot(second_all, in_part) + ff_bias
    active = jax.nn.gelu(inner).astype(BF)
    result = hidden_in + scatter_rows(dot(active, back_part)) + biases[3]
    output = from_rows(result.astype(BF))

    grad_rows = grad_low.astype(F32)
    grad_all = gather_rows(grad_low)
    grad_active = dot_nt(grad_all, back_part)
    grad_inner = jax.vjp(jax.nn.gelu, inner)[1](grad_active)[0].astype(BF)
    grad_back = dot_tn(active, grad_all)
    grad_in = dot_tn(second_all, grad_inner)
    grad_second = scatter_rows(dot_nt(grad_inner, in_part))
    grad_hidden = grad_rows + norm_back(grad_second * gains[1], normed_two, spread_two)

    grad_branch = grad_hidden.astype(BF)
    branch_all = gather_rows(grad_branch)
    grad_mixed = dot_nt(branch_all, out_part).astype(BF)
    grad_out = dot_tn(mixed, branch_all)
    grad_qkv = attend_back(rank_word, qkv, grad_mixed, logs)
    grad_first = scatter_rows(dot_nt(grad_qkv, qkv_part))
    grad_weight = dot_tn(first_all, grad_qkv)
    grad_inputs = grad_hidden + norm_back(grad_first * gains[0], normed_one, spread_one)
    grad_tokens = from_rows(grad_inputs.astype(BF))

    owned_back = scatter_lines(grad_back)
    owned_in = scatter_columns(grad_in).reshape(local, hidden)
    owned_out = scatter_lines(grad_out)
    owned_qkv = scatter_columns(grad_weight).reshape(local, ranks, groups, 3, lanes)
    owned_qkv = owned_qkv.transpose(0, 3, 1, 2, 4).reshape(local, 3 * width)

    qkv_sums = jnp.sum(grad_qkv.astype(F32), 0).reshape(groups, 3, lanes)

    def at_rank(vector, size):
        return lax.dynamic_update_slice_in_dim(jnp.zeros((size,), F32), vector, rank * vector.shape[0], 0)

    sums = jnp.stack(
        [
            jnp.sum(grad_first * normed_one, 0),
            jnp.sum(grad_second * normed_two, 0),
            jnp.sum(grad_first, 0),
            jnp.sum(grad_second, 0),
            at_rank(qkv_sums[:, 0].reshape(part), width),
            at_rank(qkv_sums[:, 2].reshape(part), width),
            jnp.sum(grad_branch.astype(F32), 0),
            jnp.sum(grad_rows, 0),
        ]
    )
    ff_sums = at_rank(jnp.sum(grad_inner.astype(F32), 0), hidden)
    sums = lax.psum((sums, ff_sums), EVERY)
    at = shard * spans + ctx
    mine = lax.dynamic_slice_in_dim(sums[0], at * (width // blocks), width // blocks, 1)
    ff_mine = lax.dynamic_slice_in_dim(sums[1], at * (hidden // blocks), hidden // blocks, 0)
    return (
        output,
        grad_tokens,
        owned_qkv,
        owned_out,
        owned_in,
        owned_back,
        mine[0:2],
        mine[2:4],
        mine[4:8],
        ff_mine,
    )


def solution(mesh):
    rows = P(("replica", "shard"), "ctx", None)
    lines, columns, flat = P(LINE, None), P(None, LINE), P(LINE)
    return jax.shard_map(
        body,
        mesh=mesh,
        in_specs=(rows, lines, lines, lines, lines, columns, columns, columns, flat, rows),
        out_specs=(rows, rows, lines, lines, lines, lines, columns, columns, columns, flat),
        check_vma=False,
    )
```

```python
import functools

import jax
import jax.numpy as jnp
from jax import lax
from jax.experimental import pallas as pl
from jax.experimental.pallas import tpu as pltpu
from jax.sharding import PartitionSpec as P

HEADS = 12
HEAD_DIM = 64
EPS = 1e-05
NEG = -1e30
BLOCK = 256
LINE = ("shard", "ctx")
EVERY = ("replica", "shard", "ctx")
BF = jnp.bfloat16
F32 = jnp.float32


def normalize(values):
    centered = values - jnp.mean(values, -1, keepdims=True)
    spread = lax.rsqrt(jnp.mean(centered * centered, -1, keepdims=True) + EPS)
    return centered * spread, spread


def norm_back(upstream, normed, spread):
    first_mean = jnp.mean(upstream, -1, keepdims=True)
    second_mean = jnp.mean(upstream * normed, -1, keepdims=True)
    return spread * (upstream - first_mean - normed * second_mean)


def dot(a, b):
    return jnp.dot(a, b, preferred_element_type=F32)


def dot_nt(a, b):
    return lax.dot_general(a, b, (((1,), (1,)), ((), ())), preferred_element_type=F32)


def dot_tn(a, b):
    return lax.dot_general(a, b, (((0,), (0,)), ((), ())), preferred_element_type=F32)


def place(rank, block, rows):
    per_rank = rows // BLOCK
    owner, part = block // per_rank, block % per_rank
    return pl.multiple_of((owner ^ rank) * rows + part * BLOCK, BLOCK)


def head_mask(lanes, head):
    lane = lax.broadcasted_iota(jnp.int32, (BLOCK, lanes), 1)
    return (lane >= head * HEAD_DIM) & (lane < (head + 1) * HEAD_DIM)


def diagonal(scores):
    key = lax.broadcasted_iota(jnp.int32, scores.shape, 0)
    query = lax.broadcasted_iota(jnp.int32, scores.shape, 1)
    return jnp.where(key <= query, scores, NEG)


def attend_kernel(rows, rank_ref, qkv_ref, mixed_ref, log_ref, keys, values_t):
    length, lanes = mixed_ref.shape
    rank = rank_ref[0]
    heads = lanes // HEAD_DIM
    for block in range(length // BLOCK):
        at = pl.ds(place(rank, block, rows), BLOCK)
        here = slice(block * BLOCK, (block + 1) * BLOCK)
        keys[here, :] = qkv_ref[at, lanes : 2 * lanes]
        values_t[:, here] = qkv_ref[at, 2 * lanes :].T
    for block in range(length // BLOCK):
        at = pl.ds(place(rank, block, rows), BLOCK)
        start, stop = block * BLOCK, (block + 1) * BLOCK
        query = qkv_ref[at, :lanes]
        parts = []
        for head in range(heads):
            one = slice(head * HEAD_DIM, (head + 1) * HEAD_DIM)
            one_query = jnp.where(head_mask(lanes, head), query, jnp.zeros_like(query))
            near = diagonal(dot_nt(keys[start:stop, :], one_query))
            highest = jnp.max(near, 0, keepdims=True)
            if block:
                far = dot_nt(keys[:start, :], one_query)
                highest = jnp.maximum(highest, jnp.max(far, 0, keepdims=True))
            near = jnp.exp(near - highest)
            total = jnp.sum(near, 0, keepdims=True)
            mixed = dot(values_t[one, start:stop], near.astype(BF))
            if block:
                far = jnp.exp(far - highest)
                total = total + jnp.sum(far, 0, keepdims=True)
                mixed = mixed + dot(values_t[one, :start], far.astype(BF))
            parts.append(mixed / total)
            log_ref[head : head + 1, start:stop] = highest + jnp.log(total)
        mixed_ref[at, :] = jnp.concatenate(parts, 0).T.astype(BF)


def attend_back_kernel(
    rows, rank_ref, qkv_ref, grad_ref, log_ref, out_ref, keys, values, keys_t, key_sum, value_sum
):
    length, lanes = grad_ref.shape
    rank = rank_ref[0]
    heads = lanes // HEAD_DIM
    scale = HEAD_DIM ** (-0.5)
    for block in range(length // BLOCK):
        at = pl.ds(place(rank, block, rows), BLOCK)
        here = slice(block * BLOCK, (block + 1) * BLOCK)
        key = qkv_ref[at, lanes : 2 * lanes]
        keys[here, :] = key
        keys_t[:, here] = key.T
        values[here, :] = qkv_ref[at, 2 * lanes :]
    for block in range(length // BLOCK):
        at = pl.ds(place(rank, block, rows), BLOCK)
        start, stop = block * BLOCK, (block + 1) * BLOCK
        query = qkv_ref[at, :lanes]
        grad = grad_ref[at, :]
        parts = []
        near_key = near_value = far_key = far_value = None
        for head in range(heads):
            one = slice(head * HEAD_DIM, (head + 1) * HEAD_DIM)
            mask = head_mask(lanes, head)
            one_query = jnp.where(mask, query, jnp.zeros_like(query))
            one_grad = jnp.where(mask, grad, jnp.zeros_like(grad))
            logs = log_ref[head : head + 1, start:stop]
            near = jnp.exp(diagonal(dot_nt(keys[start:stop, :], one_query)) - logs)
            near_grad = dot_nt(values[start:stop, :], one_grad)
            level = jnp.sum(near * near_grad, 0, keepdims=True)
            if block:
                far = jnp.exp(dot_nt(keys[:start, :], one_query) - logs)
                far_grad = dot_nt(values[:start, :], one_grad)
                level = level + jnp.sum(far * far_grad, 0, keepdims=True)
            near_low = near.astype(BF)
            near_scores = (near * (near_grad - level)).astype(BF)
            value_term, key_term = dot(near_low, one_grad), dot(near_scores, one_query)
            near_value = value_term if near_value is None else near_value + value_term
            near_key = key_term if near_key is None else near_key + key_term
            query_term = dot(keys_t[one, start:stop], near_scores)
            if block:
                far_low = far.astype(BF)
                far_scores = (far * (far_grad - level)).astype(BF)
                value_term, key_term = dot(far_low, one_grad), dot(far_scores, one_query)
                far_value = value_term if far_value is None else far_value + value_term
                far_key = key_term if far_key is None else far_key + key_term
                query_term = query_term + dot(keys_t[one, :start], far_scores)
            parts.append(query_term)
        key_sum[start:stop, :] = near_key
        value_sum[start:stop, :] = near_value
        if block:
            key_sum[:start, :] += far_key
            value_sum[:start, :] += far_value
        query_grad = jnp.concatenate(parts, 0).T.astype(BF).astype(F32) * scale
        out_ref[at, :lanes] = query_grad.astype(BF)
    for block in range(length // BLOCK):
        at = pl.ds(place(rank, block, rows), BLOCK)
        here = slice(block * BLOCK, (block + 1) * BLOCK)
        out_ref[at, lanes : 2 * lanes] = key_sum[here, :].astype(BF)
        out_ref[at, 2 * lanes :] = value_sum[here, :].astype(BF)


def attention_calls(length, rows, groups, lanes):
    heads = lanes // HEAD_DIM
    wide = pl.BlockSpec((length, 3 * lanes), lambda g, r: (0, g))
    thin = pl.BlockSpec((length, lanes), lambda g, r: (0, g))
    logs = pl.BlockSpec((None, heads, length), lambda g, r: (g, 0, 0))
    pairs = groups * heads * length * length // 2
    params = pltpu.CompilerParams(vmem_limit_bytes=56 * 2**20)
    forward = pl.pallas_call(
        functools.partial(attend_kernel, rows),
        grid_spec=pltpu.PrefetchScalarGridSpec(
            num_scalar_prefetch=1,
            grid=(groups,),
            in_specs=[wide],
            out_specs=[thin, logs],
            scratch_shapes=[pltpu.VMEM((length, lanes), BF), pltpu.VMEM((lanes, length), BF)],
        ),
        out_shape=[
            jax.ShapeDtypeStruct((length, groups * lanes), BF),
            jax.ShapeDtypeStruct((groups, heads, length), F32),
        ],
        cost_estimate=pl.CostEstimate(
            flops=pairs * 16 * HEAD_DIM, bytes_accessed=length * groups * lanes * 8, transcendentals=pairs
        ),
        compiler_params=params,
        name="attend",
    )
    backward = pl.pallas_call(
        functools.partial(attend_back_kernel, rows),
        grid_spec=pltpu.PrefetchScalarGridSpec(
            num_scalar_prefetch=1,
            grid=(groups,),
            in_specs=[wide, thin, logs],
            out_specs=wide,
            scratch_shapes=[
                pltpu.VMEM((length, lanes), BF),
                pltpu.VMEM((length, lanes), BF),
                pltpu.VMEM((lanes, length), BF),
                pltpu.VMEM((length, lanes), F32),
                pltpu.VMEM((length, lanes), F32),
            ],
        ),
        out_shape=jax.ShapeDtypeStruct((length, 3 * groups * lanes), BF),
        cost_estimate=pl.CostEstimate(
            flops=pairs * 40 * HEAD_DIM, bytes_accessed=length * groups * lanes * 14, transcendentals=pairs
        ),
        compiler_params=params,
        name="attend_back",
    )
    return forward, backward


ORDER = ((0, 1, 3, 2), (0, 3, 1, 2))


class Slots:
    def __init__(self, shapes, slot, parts):
        self.shapes, self.slot, self.parts = shapes, slot, parts

    def copies(self, where, buffers, arrays, move):
        for side in range(2):
            for other in range(2):
                cut = where[1 + side] ^ other
                for j, relative in enumerate(ORDER[side]):
                    z = where[0] ^ relative
                    for array, rows, columns, row, column in self.parts(side, cut, z):
                        low = buffers[2 * side + other].at[j, :, columns[0] : columns[1]]
                        high = arrays[array].at[pl.ds(pl.multiple_of(row, 16), rows), column[0] : column[1]]
                        move(low, high)


def slot_kernel(slots, inward, where_ref, *refs):
    count = len(slots.shapes)
    arrays, buffers = (refs[4:], refs[:4]) if inward else (refs[:count], refs[count:])

    def move(low, high):
        source, target = (low, high) if inward else (high, low)
        target[...] = source[...]

    slots.copies([where_ref[i] for i in range(3)], buffers, arrays, move)


def slot_call(slots, inward, name):
    arrays = [jax.ShapeDtypeStruct(shape, BF) for shape in slots.shapes]
    buffers = [jax.ShapeDtypeStruct((4,) + slots.slot, BF)] * 4
    given, made = (buffers, arrays) if inward else (arrays, buffers)
    size = 32 * slots.slot[0] * slots.slot[1]
    return pl.pallas_call(
        functools.partial(slot_kernel, slots, inward),
        in_specs=[pl.BlockSpec(memory_space=pltpu.SMEM)] + [pl.BlockSpec(memory_space=pltpu.VMEM)] * len(given),
        out_specs=[pl.BlockSpec(memory_space=pltpu.VMEM)] * len(made),
        out_shape=made,
        compiler_params=pltpu.CompilerParams(vmem_limit_bytes=32 * 2**20),
        cost_estimate=pl.CostEstimate(flops=0, bytes_accessed=2 * size, transcendentals=0),
        name=name,
    )


def row_moves(shards, spans, seqs):
    chips = spans // (2 * seqs)
    moves = ([], [])
    for shard in range(shards):
        for span in range(spans):
            for item in range(seqs):
                sequence = (shard % 2) * seqs + item
                rank = span // seqs
                target = (shard - shard % 2 + rank % 2) * spans + sequence * chips + rank // 2
                moves[(item + span) % 2].append((shard * spans + span, target))
    return moves


def back_moves(moves):
    return tuple([(b, a) for a, b in one] for one in moves)


def group_moves(shards, spans, ranks):
    chips = ranks // 2
    moves = []
    for k in range(1, ranks):
        one = []
        for shard in range(shards):
            for span in range(spans):
                rank = (span % chips) * 2 + shard % 2
                other = rank ^ k
                target = (shard - shard % 2 + other % 2) * spans + span - span % chips + other // 2
                one.append((shard * spans + span, target))
        moves.append(one)
    return moves


def body(
    tokens, weight_qkv, weight_out, weight_in, weight_back, gains_in, shifts_in, biases_in, ff_bias_in, cotangent
):
    seqs, span, width = tokens.shape
    shards, spans = lax.axis_size("shard"), lax.axis_size("ctx")
    shard, ctx = lax.axis_index("shard"), lax.axis_index("ctx")
    ranks = spans // seqs
    rows, length = seqs * span, spans * span
    chips = ranks // 2
    rank = (ctx % chips) * 2 + shard % 2
    core = shard % 2
    hidden = weight_back.shape[0] * shards * spans
    part, ff_part = width // ranks, hidden // ranks
    blocks = shards * spans
    heads = HEADS // ranks
    lanes = 2 * HEAD_DIM if heads % 2 == 0 else heads * HEAD_DIM
    groups = part // lanes
    scale = HEAD_DIM ** (-0.5)
    moves = row_moves(shards, spans, seqs)
    returns = back_moves(moves)
    turns = group_moves(shards, spans, ranks)
    odd_span = ctx % 2
    odd_sequence = (ctx // chips) % 2
    replicas = lax.axis_size("replica")
    paired = shards == 2 and spans == 4 and replicas == 4 and ranks == 2

    def to_rows(items):
        one = lax.ppermute(lax.dynamic_index_in_dim(items, odd_span, 0, False), LINE, moves[0])
        two = lax.ppermute(lax.dynamic_index_in_dim(items, 1 - odd_span, 0, False), LINE, moves[1])
        return jnp.where(odd_sequence == 0, jnp.concatenate([one, two]), jnp.concatenate([two, one]))

    def from_rows(low):
        items = low.reshape(seqs, span, width)
        one = lax.ppermute(lax.dynamic_index_in_dim(items, odd_sequence, 0, False), LINE, returns[0])
        two = lax.ppermute(lax.dynamic_index_in_dim(items, 1 - odd_sequence, 0, False), LINE, returns[1])
        return jnp.where(odd_span == 0, jnp.stack([one, two]), jnp.stack([two, one]))

    def gather_rows(low):
        return jnp.concatenate([low] + [lax.ppermute(low, LINE, one) for one in turns])

    def scatter_rows(partial):
        total = partial[:rows]
        for k, one in enumerate(turns):
            sent = partial[(k + 1) * rows : (k + 2) * rows].astype(BF)
            total = total + lax.ppermute(sent, LINE, one).astype(F32)
        return total

    def swap(items):
        return lax.ppermute(items, "shard", [(0, 1), (1, 0)])

    def gather_columns(weight):
        whole = lax.all_gather(weight, LINE, axis=0, tiled=True)
        return lax.dynamic_index_in_dim(whole, rank, 1, False)

    def gather_lines(weight):
        whole = lax.all_gather(weight, LINE, axis=0, tiled=True)
        size = whole.shape[0] // ranks
        return lax.dynamic_slice_in_dim(whole, rank * size, size, 0)

    def scatter_columns(grad):
        whole = jnp.zeros((grad.shape[0], ranks, grad.shape[1]), BF)
        whole = lax.dynamic_update_slice_in_dim(whole, grad[:, None], rank, 1)
        owned = lax.psum_scatter(whole, LINE, scatter_dimension=0, tiled=True)
        return lax.psum(owned, "replica").astype(F32)

    def scatter_lines(grad):
        whole = jnp.zeros((grad.shape[0] * ranks, grad.shape[1]), BF)
        whole = lax.dynamic_update_slice_in_dim(whole, grad, rank * grad.shape[0], 0)
        owned = lax.psum_scatter(whole, LINE, scatter_dimension=0, tiled=True)
        return lax.psum(owned, "replica").astype(F32)

    replica = lax.axis_index("replica")
    bits = (replica % 2, replica // 2)
    where = jnp.stack([ctx, bits[0], bits[1]]).astype(jnp.int32)

    def along_z(items, step):
        return lax.ppermute(items, "ctx", [(i, i ^ step) for i in range(4)])

    def across(items, side):
        return lax.ppermute(items, "replica", [(i, i ^ (1 + side)) for i in range(4)])

    def after(items, *others):
        return lax.optimization_barrier((items, others))[0]

    def plus(a, b):
        return (a.astype(F32) + b.astype(F32)).astype(BF)

    def spread(owns, gates=(None, None, None)):
        def gated(items, gate):
            return items if gate is None else after(items, gate)

        owns = gated(owns, gates[0])
        seen = [along_z(own, ORDER[side][1]) for side, own in enumerate(owns)]
        twos = [jnp.stack([own, one]) for own, one in zip(owns, seen)]
        twos = gated(twos, gates[1])
        far = [along_z(two, ORDER[side][2]) for side, two in enumerate(twos)]
        fours = [jnp.concatenate([two, one]) for two, one in zip(twos, far)]
        fours = gated(fours, gates[2])
        others = [across(four, side) for side, four in enumerate(fours)]
        return [fours[0], others[0], fours[1], others[1]], (twos, fours, others)

    def settle(one, other, side):
        one, other = one.astype(F32), other.astype(F32)
        return jnp.where(bits[side] == 0, jnp.concatenate([one, other]), jnp.concatenate([other, one]))

    def collect(buffers, gates=(None, None, None, None, None)):
        def gated(items, gate):
            return items if gate is None else after(items, gate)

        keeps, sends = (buffers[0], buffers[2]), (buffers[1], buffers[3])
        got = gated([across(send, side) for side, send in enumerate(sends)], gates[0])
        sends = [plus(keep[2:], one[2:]) for keep, one in zip(keeps, got)]
        keeps = [plus(keep[:2], one[:2]) for keep, one in zip(keeps, got)]
        got = gated([along_z(send, ORDER[side][2]) for side, send in enumerate(sends)], gates[1])
        sends = [plus(keep[1], one[1]) for keep, one in zip(keeps, got)]
        keeps = [plus(keep[0], one[0]) for keep, one in zip(keeps, got)]
        got = gated([along_z(send, ORDER[side][1]) for side, send in enumerate(sends)], gates[2])
        keeps = [plus(keep, one) for keep, one in zip(keeps, got)]
        got = gated([across(keep, 1 - side) for side, keep in enumerate(keeps)], gates[3])
        keeps = [plus(keep, one) for keep, one in zip(keeps, got)]
        got = gated([across(keep, side) for side, keep in enumerate(keeps)], gates[4])
        return [settle(keep, one, side) for side, (keep, one) in enumerate(zip(keeps, got))]

    def halves(items, side):
        size = items.shape[0] // 2
        return lax.dynamic_slice_in_dim(items, bits[side] * size, size, 0)

    def by_shard(weight):
        mine = lax.dynamic_index_in_dim(weight, core, 1, False)
        other = swap(lax.dynamic_index_in_dim(weight, 1 - core, 1, False))
        first, second = jnp.where(core == 0, mine, other), jnp.where(core == 0, other, mine)
        return first, second

    def to_shard(first, second):
        mine, other = jnp.where(core == 0, first, second), jnp.where(core == 0, second, first)
        other = swap(other.astype(BF)).astype(F32)
        return jnp.where(core == 0, jnp.stack([mine, other], 1), jnp.stack([other, mine], 1))

    def by_shard(weight):
        mine = lax.dynamic_index_in_dim(weight, core, 1, False)
        other = swap(lax.dynamic_index_in_dim(weight, 1 - core, 1, False))
        return jnp.where(core == 0, mine, other), jnp.where(core == 0, other, mine)

    def to_shard(first, second):
        mine, other = jnp.where(core == 0, first, second), jnp.where(core == 0, second, first)
        other = swap(other.astype(BF)).astype(F32)
        return jnp.where(core == 0, jnp.stack([mine, other], 1), jnp.stack([other, mine], 1))

    def slot_groups():
        ff_local = weight_back.shape[0]
        half, ff_half, wide = local // 2, ff_local // 2, 3 * part
        third = width // 2

        def attention_parts(side, cut, z):
            at = z * local + cut * half
            return (
                (0, half, (0, wide), side * (width // 2) + at, (0, wide)),
                (1, half, (wide, wide + third), at, (side * third, (side + 1) * third)),
            )

        def ff_parts(side, cut, z):
            at = z * ff_local + side * ff_half + cut * (ff_half // 2)
            return (
                (0, half, (0, ff_part), side * (width // 2) + z * local + cut * half, (0, ff_part)),
                (1, half, (ff_part, ff_part + width), at, (0, width)),
                (1, half, (ff_part + width, ff_part + 2 * width), at + half, (0, width)),
            )

        return (
            Slots([(width, wide), (part, width)], (half, wide + third), attention_parts),
            Slots([(width, ff_part), (ff_part, width)], (half, ff_part + 2 * width), ff_parts),
        )

    small_in = jnp.concatenate(
        [gains_in, shifts_in, biases_in, ff_bias_in.reshape(hidden // width, width // blocks)]
    )
    if paired:
        seen = jnp.stack([small_in, swap(small_in)])
        seen = jnp.concatenate([seen, along_z(seen, 1)])
        seen = jnp.concatenate([seen, along_z(seen, 3)])
        every = jnp.arange(8)
        near = ctx ^ (every % 4)
        near = jnp.where(near > 1, 5 - near, near)
        small = jnp.take(seen, 2 * near + (core ^ (every // 4)), axis=0).astype(F32)
    else:
        small = lax.all_gather(small_in, LINE, axis=0).astype(F32)
    vectors = small[:, :8].swapaxes(0, 1).reshape(8, width)
    gains, shifts, biases = vectors[0:2], vectors[2:4], vectors[4:8]
    ff_bias = lax.dynamic_slice_in_dim(small[:, 8:].reshape(hidden), rank * ff_part, ff_part, 0)

    local = weight_qkv.shape[0]
    ordered = weight_qkv.reshape(local, 3, ranks, groups, lanes).transpose(0, 2, 3, 1, 4)
    ordered = ordered.reshape(local, ranks, 3 * part)
    if paired:
        attention_slots, ff_slots = slot_groups()
        third, ff_half = width // 2, weight_back.shape[0] // 2
        owns = [
            halves(jnp.concatenate([items, weight_out[:, side * third : (side + 1) * third]], 1), side)
            for side, items in enumerate(by_shard(ordered))
        ]
        sent, (twos, fours, others) = spread(owns)
        qkv_part, out_part = slot_call(attention_slots, True, "join_attention")(where, *sent)
        owns = []
        for side, items in enumerate(by_shard(weight_in.reshape(local, ranks, ff_part))):
            lines = halves(weight_back[side * ff_half : (side + 1) * ff_half], side)
            size = lines.shape[0] // 2
            owns.append(jnp.concatenate([halves(items, side), lines[:size], lines[size:]], 1))
        sent, ff_steps = spread(owns, (twos, fours, others))
        in_part, back_part = slot_call(ff_slots, True, "join_ff")(where, *sent)
    else:
        qkv_part = gather_columns(ordered)
        out_part = gather_lines(weight_out)
        in_part = gather_columns(weight_in.reshape(local, ranks, ff_part))
        back_part = gather_lines(weight_back)

    def of_rank(vector):
        return lax.dynamic_slice_in_dim(vector, rank * part, part, 0).reshape(groups, lanes)

    none = jnp.zeros((groups, lanes), F32)
    qkv_bias = jnp.stack([of_rank(biases[0]), none, of_rank(biases[1])], 1).reshape(-1)
    qkv_scale = jnp.stack([none + scale, none + 1, none + 1], 1).reshape(-1)
    attend, attend_back = attention_calls(length, rows, groups, lanes)
    rank_word = rank.astype(jnp.int32).reshape(1)

    inputs = to_rows(tokens).astype(F32)
    if paired:
        cotangent = after(cotangent, ff_steps[1])
    grad_low = to_rows(cotangent)
    normed_one, spread_one = normalize(inputs)
    first_all = gather_rows((normed_one * gains[0] + shifts[0]).astype(BF))
    qkv = ((dot(first_all, qkv_part) + qkv_bias) * qkv_scale).astype(BF)
    mixed, logs = attend(rank_word, qkv)
    hidden_in = inputs + scatter_rows(dot(mixed, out_part)) + biases[2]
    normed_two, spread_two = normalize(hidden_in)
    second_all = gather_rows((normed_two * gains[1] + shifts[1]).astype(BF))
    inner = dot(second_all, in_part) + ff_bias
    active = jax.nn.gelu(inner).astype(BF)
    result = hidden_in + scatter_rows(dot(active, back_part)) + biases[3]
    output = from_rows(result.astype(BF))

    grad_rows = grad_low.astype(F32)
    grad_all = gather_rows(grad_low)
    grad_active = dot_nt(grad_all, back_part)
    grad_inner = jax.vjp(jax.nn.gelu, inner)[1](grad_active)[0].astype(BF)
    grad_back = dot_tn(active, grad_all).astype(BF)
    grad_in = dot_tn(second_all, grad_inner).astype(BF)
    grad_second = scatter_rows(dot_nt(grad_inner, in_part))
    grad_hidden = grad_rows + norm_back(grad_second * gains[1], normed_two, spread_two)

    grad_branch = grad_hidden.astype(BF)
    branch_all = gather_rows(grad_branch)
    grad_mixed = dot_nt(branch_all, out_part).astype(BF)
    grad_out = dot_tn(mixed, branch_all).astype(BF)
    grad_qkv = attend_back(rank_word, qkv, grad_mixed, logs)
    if paired:
        ff_owned = collect(
            slot_call(ff_slots, False, "part_ff")(where, grad_in, grad_back), (grad_mixed, grad_qkv, None, None, None)
        )
    grad_first = scatter_rows(dot_nt(grad_qkv, qkv_part))
    grad_weight = dot_tn(first_all, grad_qkv).astype(BF)
    grad_inputs = grad_hidden + norm_back(grad_first * gains[0], normed_one, spread_one)
    grad_tokens = from_rows(grad_inputs.astype(BF))

    if paired:
        wide = 3 * part
        first, second = collect(slot_call(attention_slots, False, "part_attention")(where, grad_weight, grad_out))
        owned_out = jnp.concatenate([first[:, wide:], second[:, wide:]], 1)
        owned_qkv = to_shard(first[:, :wide], second[:, :wide])
        first, second = ff_owned
        owned_in = to_shard(first[:, :ff_part], second[:, :ff_part])
        pieces = []
        for one in ff_owned:
            low, high = one[: local // 2, ff_part:], one[local // 2 :, ff_part:]
            pieces += [low[:, :width], low[:, width:], high[:, :width], high[:, width:]]
        owned_back = jnp.concatenate(pieces)
    else:
        owned_back, owned_in = scatter_lines(grad_back), scatter_columns(grad_in)
        owned_out, owned_qkv = scatter_lines(grad_out), scatter_columns(grad_weight)
    owned_in = owned_in.reshape(local, hidden)
    owned_qkv = owned_qkv.reshape(local, ranks, groups, 3, lanes)
    owned_qkv = owned_qkv.transpose(0, 3, 1, 2, 4).reshape(local, 3 * width)

    qkv_sums = jnp.sum(grad_qkv.astype(F32), 0).reshape(groups, 3, lanes)

    def at_rank(vector, size):
        return lax.dynamic_update_slice_in_dim(jnp.zeros((size,), F32), vector, rank * vector.shape[0], 0)

    sums = jnp.stack(
        [
            jnp.sum(grad_first * normed_one, 0),
            jnp.sum(grad_second * normed_two, 0),
            jnp.sum(grad_first, 0),
            jnp.sum(grad_second, 0),
            at_rank(qkv_sums[:, 0].reshape(part), width),
            at_rank(qkv_sums[:, 2].reshape(part), width),
            jnp.sum(grad_branch.astype(F32), 0),
            jnp.sum(grad_rows, 0),
        ]
    )
    ff_sums = at_rank(jnp.sum(grad_inner.astype(F32), 0), hidden)
    if paired:
        total = jnp.concatenate([sums.reshape(-1), ff_sums]).reshape(-1, 128)
        total = total + swap(total)
        total = total + along_z(total, 1)
        total = total + along_z(total, 3)
        total = total + across(total, 0)
        total = total + across(total, 1)
        total = total.reshape(-1)
        sums, ff_sums = total[: 8 * width].reshape(8, width), total[8 * width :]
    else:
        sums, ff_sums = lax.psum((sums, ff_sums), EVERY)
    at = shard * spans + ctx
    mine = lax.dynamic_slice_in_dim(sums, at * (width // blocks), width // blocks, 1)
    ff_mine = lax.dynamic_slice_in_dim(ff_sums, at * (hidden // blocks), hidden // blocks, 0)
    return (
        output,
        grad_tokens,
        owned_qkv,
        owned_out,
        owned_in,
        owned_back,
        mine[0:2],
        mine[2:4],
        mine[4:8],
        ff_mine,
    )


def solution(mesh):
    rows = P(("replica", "shard"), "ctx", None)
    lines, columns, flat = P(LINE, None), P(None, LINE), P(LINE)
    return jax.shard_map(
        body,
        mesh=mesh,
        in_specs=(rows, lines, lines, lines, lines, columns, columns, columns, flat, rows),
        out_specs=(rows, rows, lines, lines, lines, lines, columns, columns, columns, flat),
        check_vma=False,
    )
```

```python
import functools

import jax
import jax.numpy as jnp
from jax import lax
from jax.experimental import pallas as pl
from jax.experimental.pallas import tpu as pltpu
from jax.sharding import PartitionSpec as P

HEADS = 12
HEAD_DIM = 64
EPS = 1e-05
NEG = -1e30
BLOCK = 256
LINE = ("shard", "ctx")
EVERY = ("replica", "shard", "ctx")
BF = jnp.bfloat16
F32 = jnp.float32


def normalize(values):
    centered = values - jnp.mean(values, -1, keepdims=True)
    spread = lax.rsqrt(jnp.mean(centered * centered, -1, keepdims=True) + EPS)
    return centered * spread, spread


def norm_back(upstream, normed, spread):
    first_mean = jnp.mean(upstream, -1, keepdims=True)
    second_mean = jnp.mean(upstream * normed, -1, keepdims=True)
    return spread * (upstream - first_mean - normed * second_mean)


def dot(a, b):
    return jnp.dot(a, b, preferred_element_type=F32)


def dot_nt(a, b):
    return lax.dot_general(a, b, (((1,), (1,)), ((), ())), preferred_element_type=F32)


def dot_tn(a, b):
    return lax.dot_general(a, b, (((0,), (0,)), ((), ())), preferred_element_type=F32)


def place(rank, block, rows):
    per_rank = rows // BLOCK
    owner, part = block // per_rank, block % per_rank
    return pl.multiple_of((owner ^ rank) * rows + part * BLOCK, BLOCK)


def head_mask(lanes, head):
    lane = lax.broadcasted_iota(jnp.int32, (BLOCK, lanes), 1)
    return (lane >= head * HEAD_DIM) & (lane < (head + 1) * HEAD_DIM)


def diagonal(scores):
    key = lax.broadcasted_iota(jnp.int32, scores.shape, 0)
    query = lax.broadcasted_iota(jnp.int32, scores.shape, 1)
    return jnp.where(key <= query, scores, NEG)


def attend_kernel(rows, rank_ref, qkv_ref, mixed_ref, log_ref, keys, values_t):
    length, lanes = mixed_ref.shape
    rank = rank_ref[0]
    heads = lanes // HEAD_DIM
    for block in range(length // BLOCK):
        at = pl.ds(place(rank, block, rows), BLOCK)
        here = slice(block * BLOCK, (block + 1) * BLOCK)
        keys[here, :] = qkv_ref[at, lanes : 2 * lanes]
        values_t[:, here] = qkv_ref[at, 2 * lanes :].T
    for block in range(length // BLOCK):
        at = pl.ds(place(rank, block, rows), BLOCK)
        start, stop = block * BLOCK, (block + 1) * BLOCK
        query = qkv_ref[at, :lanes]
        parts = []
        for head in range(heads):
            one = slice(head * HEAD_DIM, (head + 1) * HEAD_DIM)
            one_query = jnp.where(head_mask(lanes, head), query, jnp.zeros_like(query))
            near = diagonal(dot_nt(keys[start:stop, :], one_query))
            highest = jnp.max(near, 0, keepdims=True)
            if block:
                far = dot_nt(keys[:start, :], one_query)
                highest = jnp.maximum(highest, jnp.max(far, 0, keepdims=True))
            near = jnp.exp(near - highest)
            total = jnp.sum(near, 0, keepdims=True)
            mixed = dot(values_t[one, start:stop], near.astype(BF))
            if block:
                far = jnp.exp(far - highest)
                total = total + jnp.sum(far, 0, keepdims=True)
                mixed = mixed + dot(values_t[one, :start], far.astype(BF))
            parts.append(mixed / total)
            log_ref[head : head + 1, start:stop] = highest + jnp.log(total)
        mixed_ref[at, :] = jnp.concatenate(parts, 0).T.astype(BF)


def attend_back_kernel(
    rows, rank_ref, qkv_ref, grad_ref, log_ref, out_ref, keys, values, keys_t, key_sum, value_sum
):
    length, lanes = grad_ref.shape
    rank = rank_ref[0]
    heads = lanes // HEAD_DIM
    scale = HEAD_DIM ** (-0.5)
    for block in range(length // BLOCK):
        at = pl.ds(place(rank, block, rows), BLOCK)
        here = slice(block * BLOCK, (block + 1) * BLOCK)
        key = qkv_ref[at, lanes : 2 * lanes]
        keys[here, :] = key
        keys_t[:, here] = key.T
        values[here, :] = qkv_ref[at, 2 * lanes :]
    for block in range(length // BLOCK):
        at = pl.ds(place(rank, block, rows), BLOCK)
        start, stop = block * BLOCK, (block + 1) * BLOCK
        query = qkv_ref[at, :lanes]
        grad = grad_ref[at, :]
        parts = []
        near_key = near_value = far_key = far_value = None
        for head in range(heads):
            one = slice(head * HEAD_DIM, (head + 1) * HEAD_DIM)
            mask = head_mask(lanes, head)
            one_query = jnp.where(mask, query, jnp.zeros_like(query))
            one_grad = jnp.where(mask, grad, jnp.zeros_like(grad))
            logs = log_ref[head : head + 1, start:stop]
            near = jnp.exp(diagonal(dot_nt(keys[start:stop, :], one_query)) - logs)
            near_grad = dot_nt(values[start:stop, :], one_grad)
            level = jnp.sum(near * near_grad, 0, keepdims=True)
            if block:
                far = jnp.exp(dot_nt(keys[:start, :], one_query) - logs)
                far_grad = dot_nt(values[:start, :], one_grad)
                level = level + jnp.sum(far * far_grad, 0, keepdims=True)
            near_low = near.astype(BF)
            near_scores = (near * (near_grad - level)).astype(BF)
            value_term, key_term = dot(near_low, one_grad), dot(near_scores, one_query)
            near_value = value_term if near_value is None else near_value + value_term
            near_key = key_term if near_key is None else near_key + key_term
            query_term = dot(keys_t[one, start:stop], near_scores)
            if block:
                far_low = far.astype(BF)
                far_scores = (far * (far_grad - level)).astype(BF)
                value_term, key_term = dot(far_low, one_grad), dot(far_scores, one_query)
                far_value = value_term if far_value is None else far_value + value_term
                far_key = key_term if far_key is None else far_key + key_term
                query_term = query_term + dot(keys_t[one, :start], far_scores)
            parts.append(query_term)
        key_sum[start:stop, :] = near_key
        value_sum[start:stop, :] = near_value
        if block:
            key_sum[:start, :] += far_key
            value_sum[:start, :] += far_value
        query_grad = jnp.concatenate(parts, 0).T.astype(BF).astype(F32) * scale
        out_ref[at, :lanes] = query_grad.astype(BF)
    for block in range(length // BLOCK):
        at = pl.ds(place(rank, block, rows), BLOCK)
        here = slice(block * BLOCK, (block + 1) * BLOCK)
        out_ref[at, lanes : 2 * lanes] = key_sum[here, :].astype(BF)
        out_ref[at, 2 * lanes :] = value_sum[here, :].astype(BF)


def attention_calls(length, rows, groups, lanes):
    heads = lanes // HEAD_DIM
    wide = pl.BlockSpec((length, 3 * lanes), lambda g, r: (0, g))
    thin = pl.BlockSpec((length, lanes), lambda g, r: (0, g))
    logs = pl.BlockSpec((None, heads, length), lambda g, r: (g, 0, 0))
    pairs = groups * heads * length * length // 2
    params = pltpu.CompilerParams(vmem_limit_bytes=56 * 2**20)
    forward = pl.pallas_call(
        functools.partial(attend_kernel, rows),
        grid_spec=pltpu.PrefetchScalarGridSpec(
            num_scalar_prefetch=1,
            grid=(groups,),
            in_specs=[wide],
            out_specs=[thin, logs],
            scratch_shapes=[pltpu.VMEM((length, lanes), BF), pltpu.VMEM((lanes, length), BF)],
        ),
        out_shape=[
            jax.ShapeDtypeStruct((length, groups * lanes), BF),
            jax.ShapeDtypeStruct((groups, heads, length), F32),
        ],
        cost_estimate=pl.CostEstimate(
            flops=pairs * 16 * HEAD_DIM, bytes_accessed=length * groups * lanes * 8, transcendentals=pairs
        ),
        compiler_params=params,
        name="attend",
    )
    backward = pl.pallas_call(
        functools.partial(attend_back_kernel, rows),
        grid_spec=pltpu.PrefetchScalarGridSpec(
            num_scalar_prefetch=1,
            grid=(groups,),
            in_specs=[wide, thin, logs],
            out_specs=wide,
            scratch_shapes=[
                pltpu.VMEM((length, lanes), BF),
                pltpu.VMEM((length, lanes), BF),
                pltpu.VMEM((lanes, length), BF),
                pltpu.VMEM((length, lanes), F32),
                pltpu.VMEM((length, lanes), F32),
            ],
        ),
        out_shape=jax.ShapeDtypeStruct((length, 3 * groups * lanes), BF),
        cost_estimate=pl.CostEstimate(
            flops=pairs * 40 * HEAD_DIM, bytes_accessed=length * groups * lanes * 14, transcendentals=pairs
        ),
        compiler_params=params,
        name="attend_back",
    )
    return forward, backward


class Slots:
    def __init__(self, shapes, buffers, pieces):
        self.shapes, self.buffers, self.pieces = shapes, buffers, pieces

    def copies(self, where, buffers, arrays, move):
        for buffer, index, parts in self.pieces(where):
            for array, slot_rows, slot_columns, row, columns in parts:
                one = buffers[buffer].at[(*index, pl.ds(*slot_rows), pl.ds(*slot_columns))]
                two = arrays[array].at[pl.ds(pl.multiple_of(row, 16), slot_rows[1]), pl.ds(*columns)]
                move(one, two)


def slot_kernel(slots, inward, where_ref, *refs):
    size = len(slots.buffers) if inward else len(slots.shapes)
    arrays, buffers = (refs[size:], refs[:size]) if inward else (refs[:size], refs[size:])

    def move(low, high):
        source, target = (low, high) if inward else (high, low)
        target[...] = source[...]

    slots.copies([where_ref[i] for i in range(2)], buffers, arrays, move)


def local_call(kernel, given, made, name, scalars=0):
    size = 2 * sum(2 * one.size for one in made)
    specs = [pl.BlockSpec(memory_space=pltpu.SMEM)] * scalars
    return pl.pallas_call(
        kernel,
        in_specs=specs + [pl.BlockSpec(memory_space=pltpu.VMEM)] * given,
        out_specs=[pl.BlockSpec(memory_space=pltpu.VMEM)] * len(made),
        out_shape=made,
        compiler_params=pltpu.CompilerParams(vmem_limit_bytes=40 * 2**20),
        cost_estimate=pl.CostEstimate(flops=0, bytes_accessed=size, transcendentals=0),
        name=name,
    )


def low_shape(*shape):
    return jax.ShapeDtypeStruct(shape, BF)


def slot_call(slots, inward, name):
    arrays = [low_shape(*shape) for shape in slots.shapes]
    buffers = [low_shape(*shape) for shape in slots.buffers]
    given, made = (buffers, arrays) if inward else (arrays, buffers)
    return local_call(functools.partial(slot_kernel, slots, inward), len(given), made, name, 1)


def halves_kernel(both, first, second):
    for j in range(first.shape[0]):
        first[j], second[j] = both[j, 0], both[j, 1]


def near_rows(where_ref, side, rows, far):
    bit = where_ref[1] // 2 if side == 0 else where_ref[1] % 2
    return pl.ds(pl.multiple_of((bit ^ far) * rows, 16), rows)


def widen_kernel(where_ref, both, got_first, got_second, first, second):
    rows = got_first.shape[1]
    for side, (got, out) in enumerate(((got_first, first), (got_second, second))):
        for j in range(4):
            out[j, near_rows(where_ref, side, rows, 0), :] = both[j, side]
            out[j, near_rows(where_ref, side, rows, 1), :] = got[j]


def fold_kernel(where_ref, first, got_first, second, got_second, *made):
    rows = made[0].shape[1]
    for side, (keep, got) in enumerate(((first, got_first), (second, got_second))):
        for far in range(2):
            at = near_rows(where_ref, side, rows, far)
            for j in range(4):
                made[2 * side + far][j] = (keep[j, at, :].astype(F32) + got[j, at, :].astype(F32)).astype(BF)


def pair_kernel(first, got_first, second, got_second, out):
    for j in range(first.shape[0]):
        out[j, 0] = (first[j].astype(F32) + got_first[j].astype(F32)).astype(BF)
        out[j, 1] = (second[j].astype(F32) + got_second[j].astype(F32)).astype(BF)


def stack_kernel(*refs):
    for j, ref in enumerate(refs[:-1]):
        refs[-1][j] = ref[...]


def relay_kernel(to_x, to_y, for_y, for_x, out_x, out_y):
    out_x[:2] = to_x[:2]
    out_x[2:] = (to_x[2:].astype(F32) + for_x[...].astype(F32)).astype(BF)
    out_y[:2] = (to_y[:2].astype(F32) + for_y[...].astype(F32)).astype(BF)
    out_y[2:] = to_y[2:]


def split_kernel(own, by_x, by_y, vectors, *made):
    for j, out in enumerate(made):
        columns = own.shape[2]
        out[:, :columns] = (own[j].astype(F32) + by_x[j].astype(F32) + by_y[j].astype(F32)).astype(BF)
        out[:, columns:] = vectors[...]


def row_moves(shards, spans, seqs):
    chips = spans // (2 * seqs)
    moves = ([], [])
    for shard in range(shards):
        for span in range(spans):
            for item in range(seqs):
                sequence = (shard % 2) * seqs + item
                rank = span // seqs
                target = (shard - shard % 2 + rank % 2) * spans + sequence * chips + rank // 2
                moves[(item + span) % 2].append((shard * spans + span, target))
    return moves


def back_moves(moves):
    return tuple([(b, a) for a, b in one] for one in moves)


def group_moves(shards, spans, ranks):
    chips = ranks // 2
    moves = []
    for k in range(1, ranks):
        one = []
        for shard in range(shards):
            for span in range(spans):
                rank = (span % chips) * 2 + shard % 2
                other = rank ^ k
                target = (shard - shard % 2 + other % 2) * spans + span - span % chips + other // 2
                one.append((shard * spans + span, target))
        moves.append(one)
    return moves


def body(
    tokens, weight_qkv, weight_out, weight_in, weight_back, gains_in, shifts_in, biases_in, ff_bias_in, cotangent
):
    seqs, span, width = tokens.shape
    shards, spans = lax.axis_size("shard"), lax.axis_size("ctx")
    shard, ctx = lax.axis_index("shard"), lax.axis_index("ctx")
    ranks = spans // seqs
    rows, length = seqs * span, spans * span
    chips = ranks // 2
    rank = (ctx % chips) * 2 + shard % 2
    core = shard % 2
    hidden = weight_back.shape[0] * shards * spans
    part, ff_part = width // ranks, hidden // ranks
    blocks = shards * spans
    heads = HEADS // ranks
    local = weight_qkv.shape[0]
    lanes = 2 * HEAD_DIM if heads % 2 == 0 else heads * HEAD_DIM
    groups = part // lanes
    scale = HEAD_DIM ** (-0.5)
    moves = row_moves(shards, spans, seqs)
    returns = back_moves(moves)
    turns = group_moves(shards, spans, ranks)
    odd_span = ctx % 2
    odd_sequence = (ctx // chips) % 2
    replicas = lax.axis_size("replica")
    paired = shards == 2 and spans == 4 and replicas == 4 and ranks == 2

    def row_parts(items):
        one = lax.ppermute(lax.dynamic_index_in_dim(items, odd_span, 0, False), LINE, moves[0])
        two = lax.ppermute(lax.dynamic_index_in_dim(items, 1 - odd_span, 0, False), LINE, moves[1])
        return one, two

    def to_rows(one, two):
        return jnp.where(odd_sequence == 0, jnp.concatenate([one, two]), jnp.concatenate([two, one]))

    def from_rows(low):
        items = low.reshape(seqs, span, width)
        one = lax.ppermute(lax.dynamic_index_in_dim(items, odd_sequence, 0, False), LINE, returns[0])
        two = lax.ppermute(lax.dynamic_index_in_dim(items, 1 - odd_sequence, 0, False), LINE, returns[1])
        return jnp.where(odd_span == 0, jnp.stack([one, two]), jnp.stack([two, one]))

    def gather_rows(low):
        return jnp.concatenate([low] + [lax.ppermute(low, LINE, one) for one in turns])

    def scatter_rows(items, product):
        got = []
        for k, one in enumerate(turns):
            sent = product(items[(k + 1) * rows : (k + 2) * rows]).astype(BF)
            got.append(lax.ppermute(sent, LINE, one))
        total = product(items[:rows])
        for one in got:
            total = total + one.astype(F32)
        return total

    def swap(items):
        return lax.ppermute(items, "shard", [(0, 1), (1, 0)])

    def gather_columns(weight):
        whole = lax.all_gather(weight, LINE, axis=0, tiled=True)
        return lax.dynamic_index_in_dim(whole, rank, 1, False)

    def gather_lines(weight):
        whole = lax.all_gather(weight, LINE, axis=0, tiled=True)
        size = whole.shape[0] // ranks
        return lax.dynamic_slice_in_dim(whole, rank * size, size, 0)

    def scatter_columns(grad):
        whole = jnp.zeros((grad.shape[0], ranks, grad.shape[1]), BF)
        whole = lax.dynamic_update_slice_in_dim(whole, grad[:, None], rank, 1)
        owned = lax.psum_scatter(whole, LINE, scatter_dimension=0, tiled=True)
        return lax.psum(owned, "replica").astype(F32)

    def scatter_lines(grad):
        whole = jnp.zeros((grad.shape[0] * ranks, grad.shape[1]), BF)
        whole = lax.dynamic_update_slice_in_dim(whole, grad, rank * grad.shape[0], 0)
        owned = lax.psum_scatter(whole, LINE, scatter_dimension=0, tiled=True)
        return lax.psum(owned, "replica").astype(F32)

    replica = lax.axis_index("replica")
    where = jnp.stack([ctx, replica]).astype(jnp.int32)

    def along_z(items, step):
        return lax.ppermute(items, "ctx", [(i, i ^ step) for i in range(4)])

    def across(items, step):
        return lax.ppermute(items, "replica", [(i, i ^ step) for i in range(4)])

    def after(items, *others):
        return lax.optimization_barrier((items, others))[0] if paired else items

    def z_moves(own):
        return [along_z(own, step) for step in (1, 2, 3)]

    def stacked(own, seen, name):
        return local_call(stack_kernel, 4, [low_shape(4, *own.shape)], name)(own, *seen)[0]

    def xy_moves(four):
        return across(four, 1), across(four, 2)

    def relay_parts(by_x, by_y):
        return by_x[:2], by_y[2:]

    def relays(for_y, for_x):
        return across(for_y, 2), across(for_x, 1)

    def relayed(buffers, got, name):
        shape = low_shape(*buffers[0].shape)
        return local_call(relay_kernel, 4, [shape] * 2, name)(buffers[1], buffers[2], *got)

    def split(own, got, vectors, name):
        shape = low_shape(own.shape[1], own.shape[2] + vectors.shape[1])
        return local_call(split_kernel, 4, [shape] * 4, name)(own, *got, vectors)

    def z_sum(own, got):
        return (own.astype(F32) + got[0].astype(F32) + got[1].astype(F32) + got[2].astype(F32)).astype(BF)

    def plus(a, b):
        return (a.astype(F32) + b.astype(F32)).astype(BF)

    def by_quarters(one, got):
        one, by_x, by_y, by_both = [i.astype(F32) for i in (one, *got)]
        quarters = []
        for quarter in range(4):
            step = replica ^ quarter
            near = jnp.where(step == 0, one, by_x)
            quarters.append(jnp.where(step < 2, near, jnp.where(step == 2, by_y, by_both)))
        return quarters

    bits = (replica % 2, replica // 2)

    def of_core(weight, kinds, one_core):
        size = weight.shape[1] // (kinds * ranks)
        starts = [(kind * ranks + one_core) * size for kind in range(kinds)]
        return jnp.concatenate([lax.dynamic_slice_in_dim(weight, at, size, 1) for at in starts], 1)

    def by_halves(weight, kinds):
        mine, other = of_core(weight, kinds, core), swap(of_core(weight, kinds, 1 - core))
        blocks_of = jnp.where(core == 0, mine, other), jnp.where(core == 0, other, mine)
        return [
            lax.dynamic_slice_in_dim(one, bit * (local // 2), local // 2, 0) for one, bit in zip(blocks_of, bits)
        ]

    def by_quarter(weight, kinds):
        mine, other = of_core(weight, kinds, core), swap(of_core(weight, kinds, 1 - core))
        chosen = jnp.where(core == replica // 2, mine, other)
        return lax.dynamic_slice_in_dim(chosen, (replica % 2) * (local // 2), local // 2, 0)

    def to_shard(first, second):
        mine, other = jnp.where(core == 0, first, second), jnp.where(core == 0, second, first)
        other = swap(other.astype(BF)).astype(F32)
        return jnp.where(core == 0, mine, other), jnp.where(core == 0, other, mine)

    def slot_groups():
        ff_local = weight_back.shape[0]
        half, ff_half, wide = local // 2, ff_local // 2, 3 * part
        third = width // 2

        def attention_pieces(where):
            for buffer, (step, first, count) in enumerate(((0, 0, 4), (1, 0, 4), (2, 0, 4), (3, 0, 2), (3, 2, 2))):
                quarter = where[1] ^ step
                for j in range(count):
                    at = (where[0] ^ (first + j)) * local + (quarter % 2) * half
                    column = pl.multiple_of((quarter // 2) * third, 128)
                    parts = [(1, (0, half), (wide, third), at, (column, third))]
                    for group in range(groups):
                        for kind in range(3):
                            low, high = kind * part + group * lanes, (3 * group + kind) * lanes
                            row = (quarter // 2) * third + at
                            parts.append((0, (0, half), (low, lanes), row, (high, lanes)))
                    yield buffer, (j,), parts

        def ff_parts(side, cut, z):
            at = side * third + z * local + cut * half
            row = z * ff_local + side * ff_half + cut * (ff_half // 2)
            return (
                (0, (0, half), (0, width), at, (0, width)),
                (0, (half, half), (0, width), at, (width, width)),
                (1, (2 * half, ff_half // 2), (0, width), row, (0, width)),
            )

        def ff_pieces(where):
            for side, bit in enumerate((where[1] % 2, where[1] // 2)):
                for z in range(4):
                    yield 2 * side, (z,), ff_parts(side, bit, z)
                    yield 2 * side + 1, (z,), ff_parts(side, 1 - bit, z)

        attention = (half, wide + third)
        feed = (2 * half + ff_half // 2, width)
        shapes = [(width, ff_part), (ff_part, width)]
        return (
            Slots([(width, wide), (part, width)], [(n, *attention) for n in (4, 4, 4, 2, 2)], attention_pieces),
            Slots(shapes, [(4, *feed)] * 4, ff_pieces),
        )

    small_in = jnp.concatenate(
        [gains_in, shifts_in, biases_in, ff_bias_in.reshape(hidden // width, width // blocks)]
    )
    if paired:
        attention_slots, ff_slots = slot_groups()
        half, third = local // 2, width // 2
        small_near = swap(small_in)
        lines = lax.dynamic_slice(weight_out, ((replica % 2) * half, (replica // 2) * third), (half, third))
        own = jnp.concatenate([by_quarter(weight_qkv, 3), lines], 1)
        seen = z_moves(own)
        owns = []
        ff_quarter = weight_back.shape[0] // 4
        for side, one in enumerate(by_halves(after(weight_in, own), 1)):
            at = (2 * side + bits[side]) * ff_quarter
            lines = lax.dynamic_slice_in_dim(weight_back, at, ff_quarter, 0)
            owns.append(jnp.where(bits[1 - side] == 0, jnp.concatenate([one[:, :width], one[:, width:]]), lines))
        owns = jnp.stack(owns)
        ff_own = lax.all_gather(owns, "ctx", axis=0)
        seen_small = after(jnp.stack([small_in, small_near]), own)
        seen_small = jnp.concatenate([seen_small] + [along_z(seen_small, step) for step in (1, 2, 3)])
        four = stacked(own, after(seen, (owns, seen_small)), "stack_attention")
        xy = xy_moves(four)
        token_parts = after(row_parts(tokens), four)
        pieces = relay_parts(*xy)
        relay = relays(*pieces)
        qkv_part, out_part = slot_call(attention_slots, True, "join_attention")(where, four, *xy, *relay)
    else:
        ordered = weight_qkv.reshape(local, 3, ranks, groups, lanes).transpose(0, 2, 3, 1, 4)
        qkv_part = gather_columns(ordered.reshape(local, ranks, 3 * part))
        out_part = gather_lines(weight_out)
        in_part = gather_columns(weight_in.reshape(local, ranks, ff_part))
        back_part = gather_lines(weight_back)
        token_parts = row_parts(tokens)

    if paired:
        every = jnp.arange(8)
        near = ctx ^ (every % 4)
        small = jnp.take(seen_small, 2 * near + (core ^ (every // 4)), axis=0).astype(F32)
    else:
        small = lax.all_gather(small_in, LINE, axis=0).astype(F32)
    vectors = small[:, :8].swapaxes(0, 1).reshape(8, width)
    gains, shifts, biases = vectors[0:2], vectors[2:4], vectors[4:8]
    ff_bias = lax.dynamic_slice_in_dim(small[:, 8:].reshape(hidden), rank * ff_part, ff_part, 0)

    def of_rank(vector):
        return lax.dynamic_slice_in_dim(vector, rank * part, part, 0).reshape(groups, lanes)

    none = jnp.zeros((groups, lanes), F32)
    qkv_bias = jnp.stack([of_rank(biases[0]), none, of_rank(biases[1])], 1).reshape(-1)
    qkv_scale = jnp.stack([none + scale, none + 1, none + 1], 1).reshape(-1)
    attend, attend_back = attention_calls(length, rows, groups, lanes)
    rank_word = rank.astype(jnp.int32).reshape(1)

    inputs = to_rows(*token_parts).astype(F32)
    normed_one, spread_one = normalize(inputs)
    first_all = gather_rows((normed_one * gains[0] + shifts[0]).astype(BF))
    if paired:
        quarters = [low_shape(4, *owns.shape[1:])] * 2
        ff_near = local_call(halves_kernel, 1, quarters, "halves_ff")(after(ff_own, qkv_part))
        ff_got = across(ff_near[0], 2), across(ff_near[1], 1)
        first_all = after(first_all, ff_near)
    qkv = ((dot(first_all, qkv_part) + qkv_bias) * qkv_scale).astype(BF)
    mixed, logs = attend(rank_word, qkv)
    if paired:
        halves = [low_shape(4, 2 * owns.shape[1], width)] * 2
        ff_near = local_call(widen_kernel, 3, halves, "widen_ff", 1)(where, ff_own, *after(ff_got, mixed))
        ff_far = across(ff_near[0], 1), across(ff_near[1], 2)
        mixed = after(mixed, ff_near)
        cotangent = after(cotangent, ff_near)
    cotangent_parts = row_parts(cotangent)
    hidden_in = inputs + scatter_rows(mixed, lambda one: dot(one, out_part)) + biases[2]
    normed_two, spread_two = normalize(hidden_in)
    second = (normed_two * gains[1] + shifts[1]).astype(BF)
    second_all = gather_rows(second)
    if paired:
        in_part, back_part = slot_call(ff_slots, True, "join_ff")(
            where, ff_near[0], after(ff_far[0], second), ff_near[1], after(ff_far[1], second)
        )
    inner = dot(second_all, in_part) + ff_bias
    active = jax.nn.gelu(inner).astype(BF)
    grad_low = to_rows(*after(cotangent_parts, active))
    result = hidden_in + scatter_rows(active, lambda one: dot(one, back_part)) + biases[3]
    output = from_rows(result.astype(BF))

    grad_rows = grad_low.astype(F32)
    grad_all = gather_rows(grad_low)
    grad_active = dot_nt(grad_all, back_part)
    grad_inner = jax.vjp(jax.nn.gelu, inner)[1](grad_active)[0].astype(BF)
    grad_back = dot_tn(active, grad_all).astype(BF)
    grad_in = dot_tn(second_all, grad_inner).astype(BF)
    if paired:
        ff_buffers = slot_call(ff_slots, False, "part_ff")(where, grad_in, grad_back)
        ff_got = across(ff_buffers[1], 1), across(ff_buffers[3], 2)
        grad_inner = after(grad_inner, ff_buffers)
    grad_second = scatter_rows(grad_inner, lambda one: dot_nt(one, in_part))
    grad_hidden = grad_rows + norm_back(grad_second * gains[1], normed_two, spread_two)

    grad_branch = grad_hidden.astype(BF)
    branch_all = gather_rows(grad_branch)
    grad_mixed = dot_nt(branch_all, out_part).astype(BF)
    if paired:
        ff_sums = local_call(fold_kernel, 4, quarters * 2, "fold_ff", 1)(
            where, ff_buffers[0], *after((ff_got[0], ff_buffers[2], ff_got[1]), branch_all)
        )
        ff_got = across(ff_sums[1], 2), across(ff_sums[3], 1)
        grad_mixed = after(grad_mixed, ff_sums)
    grad_qkv = attend_back(rank_word, qkv, grad_mixed, logs)
    if paired:
        ff_got = after(ff_got, (grad_qkv, output))
        ff_sums = local_call(pair_kernel, 4, [low_shape(4, 2, *ff_sums[0].shape[1:])], "add_ff")(
            ff_sums[0], ff_got[0], ff_sums[2], ff_got[1]
        )[0]
        grad_qkv = after(grad_qkv, ff_sums)
        ff_one = lax.psum_scatter(
            ff_sums.reshape(-1, width), "ctx", scatter_dimension=0, tiled=True
        ).reshape(ff_sums.shape[1:])
    grad_first = scatter_rows(grad_qkv, lambda one: dot_nt(one, qkv_part))
    grad_out = dot_tn(mixed, branch_all).astype(BF)
    grad_weight = dot_tn(first_all, grad_qkv).astype(BF)
    if paired:
        buffers = slot_call(attention_slots, False, "part_attention")(where, grad_weight, grad_out)
        got = across(buffers[3], 1), across(buffers[4], 2)
        grad_first = after(grad_first, buffers)
    grad_inputs = grad_hidden + norm_back(grad_first * gains[0], normed_one, spread_one)
    grad_tokens_low = grad_inputs.astype(BF)
    grad_tokens = from_rows(grad_tokens_low)

    grad_second_late, grad_branch, grad_rows, grad_inner = after(
        (grad_second, grad_branch, grad_rows, grad_inner), grad_weight
    )
    qkv_sums = jnp.sum(grad_qkv.astype(F32), 0).reshape(groups, 3, lanes)

    def at_rank(vector, size):
        return lax.dynamic_update_slice_in_dim(jnp.zeros((size,), F32), vector, rank * vector.shape[0], 0)

    sums = jnp.stack(
        [
            jnp.sum(grad_first * normed_one, 0),
            jnp.sum(grad_second_late * normed_two, 0),
            jnp.sum(grad_first, 0),
            jnp.sum(grad_second_late, 0),
            at_rank(qkv_sums[:, 0].reshape(part), width),
            at_rank(qkv_sums[:, 2].reshape(part), width),
            jnp.sum(grad_branch.astype(F32), 0),
            jnp.sum(grad_rows, 0),
        ]
    )
    ff_sums_of = at_rank(jnp.sum(grad_inner.astype(F32), 0), hidden)
    if paired:
        wide = 3 * part
        sent = relayed(buffers, after(got, grad_tokens_low), "relay_attention")
        got = across(sent[0], 1), across(sent[1], 2)
        vectors = jnp.concatenate([sums.reshape(-1), ff_sums_of.reshape(-1)]).astype(BF)
        lane_block = 128 * (-(-vectors.size // (128 * (local // 2))))
        vectors = jnp.pad(vectors, (0, lane_block * (local // 2) - vectors.size)).reshape(local // 2, lane_block)
        parts = split(buffers[0], after(got, ff_one), vectors, "split_attention")
        got = [along_z(parts[step], step) for step in (1, 2, 3)]
        ff_got = across(ff_one[0], 2), across(ff_one[1], 1)
        ff_halves = []
        for bit, mine, other in zip(bits[::-1], ff_one, ff_got):
            ff_halves.append(jnp.where(bit == 0, jnp.concatenate([mine, other]), jnp.concatenate([other, mine])))
        ff_got = across(ff_halves[0], 1), across(ff_halves[1], 2)
        ff_owned = []
        for bit, mine, other in zip(bits, ff_halves, ff_got):
            mine, other = mine.astype(F32), other.astype(F32)
            ff_owned.append((jnp.where(bit == 0, mine, other), jnp.where(bit == 0, other, mine)))
        one = z_sum(parts[0], after(got, (grad_tokens, ff_one)))
        quarters = by_quarters(one, [across(one, step) for step in (1, 2, 3)])
        vectors = [i[:, wide + third :] for i in quarters]
        vectors = vectors[0] + vectors[1] + vectors[2] + vectors[3]
        joined = [jnp.concatenate(quarters[:2]), jnp.concatenate(quarters[2:])]
        owned_out = jnp.concatenate([one[:, wide : wide + third] for one in joined], 1)
        low, high = to_shard(*[one[:, :wide] for one in joined])
        owned_qkv = [i[:, kind * part : (kind + 1) * part] for kind in range(3) for i in (low, high)]
        owned_qkv = jnp.concatenate(owned_qkv, 1)
        half = local // 2
        blocks_in = [
            jnp.concatenate([jnp.concatenate([cut[:half], cut[half : 2 * half]], 1) for cut in one]) for one in ff_owned
        ]
        owned_in = jnp.concatenate(to_shard(*blocks_in), 1)
        owned_back = jnp.concatenate([cut[2 * half :] for one in ff_owned for cut in one])
    else:
        owned_back, owned_in = scatter_lines(grad_back), scatter_columns(grad_in).reshape(local, hidden)
        owned_out, owned_qkv = scatter_lines(grad_out), scatter_columns(grad_weight)
        owned_qkv = owned_qkv.reshape(local, ranks, groups, 3, lanes)
        owned_qkv = owned_qkv.transpose(0, 3, 1, 2, 4).reshape(local, 3 * width)

    if paired:
        total = (vectors + swap(vectors)).reshape(-1)
        sums, ff_sums_of = total[: 8 * width].reshape(8, width), total[8 * width : 8 * width + hidden]
    else:
        sums, ff_sums_of = lax.psum((sums, ff_sums_of), EVERY)
    at = shard * spans + ctx
    mine = lax.dynamic_slice_in_dim(sums, at * (width // blocks), width // blocks, 1)
    ff_mine = lax.dynamic_slice_in_dim(ff_sums_of, at * (hidden // blocks), hidden // blocks, 0)
    return (
        output,
        grad_tokens,
        owned_qkv,
        owned_out,
        owned_in,
        owned_back,
        mine[0:2],
        mine[2:4],
        mine[4:8],
        ff_mine,
    )


def solution(mesh):
    rows = P(("replica", "shard"), "ctx", None)
    lines, columns, flat = P(LINE, None), P(None, LINE), P(LINE)
    return jax.shard_map(
        body,
        mesh=mesh,
        in_specs=(rows, lines, lines, lines, lines, columns, columns, columns, flat, rows),
        out_specs=(rows, rows, lines, lines, lines, lines, columns, columns, columns, flat),
        check_vma=False,
    )
```

```python
import functools

import jax
import jax.numpy as jnp
from jax import lax
from jax.experimental import pallas as pl
from jax.experimental.pallas import tpu as pltpu
from jax.sharding import PartitionSpec as P

HEADS = 12
HEAD_DIM = 64
EPS = 1e-05
NEG = -1e30
BLOCK = 256
LINE = ("shard", "ctx")
EVERY = ("replica", "shard", "ctx")
BF = jnp.bfloat16
F32 = jnp.float32


def normalize(values):
    centered = values - jnp.mean(values, -1, keepdims=True)
    spread = lax.rsqrt(jnp.mean(centered * centered, -1, keepdims=True) + EPS)
    return centered * spread, spread


def norm_back(upstream, normed, spread):
    first_mean = jnp.mean(upstream, -1, keepdims=True)
    second_mean = jnp.mean(upstream * normed, -1, keepdims=True)
    return spread * (upstream - first_mean - normed * second_mean)


def dot(a, b):
    return jnp.dot(a, b, preferred_element_type=F32)


def dot_nt(a, b):
    return lax.dot_general(a, b, (((1,), (1,)), ((), ())), preferred_element_type=F32)


def dot_tn(a, b):
    return lax.dot_general(a, b, (((0,), (0,)), ((), ())), preferred_element_type=F32)


def place(rank, block, rows):
    per_rank = rows // BLOCK
    owner, part = block // per_rank, block % per_rank
    return pl.multiple_of((owner ^ rank) * rows + part * BLOCK, BLOCK)


def head_mask(lanes, head):
    lane = lax.broadcasted_iota(jnp.int32, (BLOCK, lanes), 1)
    return (lane >= head * HEAD_DIM) & (lane < (head + 1) * HEAD_DIM)


def diagonal(scores):
    key = lax.broadcasted_iota(jnp.int32, scores.shape, 0)
    query = lax.broadcasted_iota(jnp.int32, scores.shape, 1)
    return jnp.where(key <= query, scores, NEG)


def attend_kernel(rows, rank_ref, qkv_ref, mixed_ref, log_ref, keys, values_t):
    length, lanes = mixed_ref.shape
    rank = rank_ref[0]
    heads = lanes // HEAD_DIM
    for block in range(length // BLOCK):
        at = pl.ds(place(rank, block, rows), BLOCK)
        here = slice(block * BLOCK, (block + 1) * BLOCK)
        keys[here, :] = qkv_ref[at, lanes : 2 * lanes]
        values_t[:, here] = qkv_ref[at, 2 * lanes :].T
    for block in range(length // BLOCK):
        at = pl.ds(place(rank, block, rows), BLOCK)
        start, stop = block * BLOCK, (block + 1) * BLOCK
        query = qkv_ref[at, :lanes]
        parts = []
        for head in range(heads):
            one = slice(head * HEAD_DIM, (head + 1) * HEAD_DIM)
            one_query = jnp.where(head_mask(lanes, head), query, jnp.zeros_like(query))
            near = diagonal(dot_nt(keys[start:stop, :], one_query))
            highest = jnp.max(near, 0, keepdims=True)
            if block:
                far = dot_nt(keys[:start, :], one_query)
                highest = jnp.maximum(highest, jnp.max(far, 0, keepdims=True))
            near = jnp.exp(near - highest)
            total = jnp.sum(near, 0, keepdims=True)
            mixed = dot(values_t[one, start:stop], near.astype(BF))
            if block:
                far = jnp.exp(far - highest)
                total = total + jnp.sum(far, 0, keepdims=True)
                mixed = mixed + dot(values_t[one, :start], far.astype(BF))
            parts.append(mixed / total)
            log_ref[head : head + 1, start:stop] = highest + jnp.log(total)
        mixed_ref[at, :] = jnp.concatenate(parts, 0).T.astype(BF)


def attend_back_kernel(
    rows, rank_ref, qkv_ref, grad_ref, log_ref, out_ref, keys, values, keys_t, key_sum, value_sum
):
    length, lanes = grad_ref.shape
    rank = rank_ref[0]
    heads = lanes // HEAD_DIM
    scale = HEAD_DIM ** (-0.5)
    for block in range(length // BLOCK):
        at = pl.ds(place(rank, block, rows), BLOCK)
        here = slice(block * BLOCK, (block + 1) * BLOCK)
        key = qkv_ref[at, lanes : 2 * lanes]
        keys[here, :] = key
        keys_t[:, here] = key.T
        values[here, :] = qkv_ref[at, 2 * lanes :]
    for block in range(length // BLOCK):
        at = pl.ds(place(rank, block, rows), BLOCK)
        start, stop = block * BLOCK, (block + 1) * BLOCK
        query = qkv_ref[at, :lanes]
        grad = grad_ref[at, :]
        parts = []
        near_key = near_value = far_key = far_value = None
        for head in range(heads):
            one = slice(head * HEAD_DIM, (head + 1) * HEAD_DIM)
            mask = head_mask(lanes, head)
            one_query = jnp.where(mask, query, jnp.zeros_like(query))
            one_grad = jnp.where(mask, grad, jnp.zeros_like(grad))
            logs = log_ref[head : head + 1, start:stop]
            near = jnp.exp(diagonal(dot_nt(keys[start:stop, :], one_query)) - logs)
            near_grad = dot_nt(values[start:stop, :], one_grad)
            level = jnp.sum(near * near_grad, 0, keepdims=True)
            if block:
                far = jnp.exp(dot_nt(keys[:start, :], one_query) - logs)
                far_grad = dot_nt(values[:start, :], one_grad)
                level = level + jnp.sum(far * far_grad, 0, keepdims=True)
            near_low = near.astype(BF)
            near_scores = (near * (near_grad - level)).astype(BF)
            value_term, key_term = dot(near_low, one_grad), dot(near_scores, one_query)
            near_value = value_term if near_value is None else near_value + value_term
            near_key = key_term if near_key is None else near_key + key_term
            query_term = dot(keys_t[one, start:stop], near_scores)
            if block:
                far_low = far.astype(BF)
                far_scores = (far * (far_grad - level)).astype(BF)
                value_term, key_term = dot(far_low, one_grad), dot(far_scores, one_query)
                far_value = value_term if far_value is None else far_value + value_term
                far_key = key_term if far_key is None else far_key + key_term
                query_term = query_term + dot(keys_t[one, :start], far_scores)
            parts.append(query_term)
        key_sum[start:stop, :] = near_key
        value_sum[start:stop, :] = near_value
        if block:
            key_sum[:start, :] += far_key
            value_sum[:start, :] += far_value
        query_grad = jnp.concatenate(parts, 0).T.astype(BF).astype(F32) * scale
        out_ref[at, :lanes] = query_grad.astype(BF)
    for block in range(length // BLOCK):
        at = pl.ds(place(rank, block, rows), BLOCK)
        here = slice(block * BLOCK, (block + 1) * BLOCK)
        out_ref[at, lanes : 2 * lanes] = key_sum[here, :].astype(BF)
        out_ref[at, 2 * lanes :] = value_sum[here, :].astype(BF)


def attention_calls(length, rows, groups, lanes):
    heads = lanes // HEAD_DIM
    wide = pl.BlockSpec((length, 3 * lanes), lambda g, r: (0, g))
    thin = pl.BlockSpec((length, lanes), lambda g, r: (0, g))
    logs = pl.BlockSpec((None, heads, length), lambda g, r: (g, 0, 0))
    pairs = groups * heads * length * length // 2
    params = pltpu.CompilerParams(vmem_limit_bytes=56 * 2**20)
    forward = pl.pallas_call(
        functools.partial(attend_kernel, rows),
        grid_spec=pltpu.PrefetchScalarGridSpec(
            num_scalar_prefetch=1,
            grid=(groups,),
            in_specs=[wide],
            out_specs=[thin, logs],
            scratch_shapes=[pltpu.VMEM((length, lanes), BF), pltpu.VMEM((lanes, length), BF)],
        ),
        out_shape=[
            jax.ShapeDtypeStruct((length, groups * lanes), BF),
            jax.ShapeDtypeStruct((groups, heads, length), F32),
        ],
        cost_estimate=pl.CostEstimate(
            flops=pairs * 16 * HEAD_DIM, bytes_accessed=length * groups * lanes * 8, transcendentals=pairs
        ),
        compiler_params=params,
        name="attend",
    )
    backward = pl.pallas_call(
        functools.partial(attend_back_kernel, rows),
        grid_spec=pltpu.PrefetchScalarGridSpec(
            num_scalar_prefetch=1,
            grid=(groups,),
            in_specs=[wide, thin, logs],
            out_specs=wide,
            scratch_shapes=[
                pltpu.VMEM((length, lanes), BF),
                pltpu.VMEM((length, lanes), BF),
                pltpu.VMEM((lanes, length), BF),
                pltpu.VMEM((length, lanes), F32),
                pltpu.VMEM((length, lanes), F32),
            ],
        ),
        out_shape=jax.ShapeDtypeStruct((length, 3 * groups * lanes), BF),
        cost_estimate=pl.CostEstimate(
            flops=pairs * 40 * HEAD_DIM, bytes_accessed=length * groups * lanes * 14, transcendentals=pairs
        ),
        compiler_params=params,
        name="attend_back",
    )
    return forward, backward


class Slots:
    def __init__(self, shapes, buffers, pieces):
        self.shapes, self.buffers, self.pieces = shapes, buffers, pieces

    def copies(self, where, buffers, arrays, move):
        for buffer, index, parts in self.pieces(where):
            for array, slot_rows, slot_columns, row, columns in parts:
                one = buffers[buffer].at[(*index, pl.ds(*slot_rows), pl.ds(*slot_columns))]
                two = arrays[array].at[pl.ds(pl.multiple_of(row, 16), slot_rows[1]), pl.ds(*columns)]
                move(one, two)


def slot_kernel(slots, inward, where_ref, *refs):
    size = len(slots.buffers) if inward else len(slots.shapes)
    arrays, buffers = (refs[size:], refs[:size]) if inward else (refs[:size], refs[size:])

    def move(low, high):
        source, target = (low, high) if inward else (high, low)
        target[...] = source[...]

    slots.copies([where_ref[i] for i in range(2)], buffers, arrays, move)


def local_call(kernel, given, made, name, scalars=0):
    size = 2 * sum(2 * one.size for one in made)
    specs = [pl.BlockSpec(memory_space=pltpu.SMEM)] * scalars
    return pl.pallas_call(
        kernel,
        in_specs=specs + [pl.BlockSpec(memory_space=pltpu.VMEM)] * given,
        out_specs=[pl.BlockSpec(memory_space=pltpu.VMEM)] * len(made),
        out_shape=made,
        compiler_params=pltpu.CompilerParams(vmem_limit_bytes=40 * 2**20),
        cost_estimate=pl.CostEstimate(flops=0, bytes_accessed=size, transcendentals=0),
        name=name,
    )


def low_shape(*shape):
    return jax.ShapeDtypeStruct(shape, BF)


def slot_call(slots, inward, name):
    arrays = [low_shape(*shape) for shape in slots.shapes]
    buffers = [low_shape(*shape) for shape in slots.buffers]
    given, made = (buffers, arrays) if inward else (arrays, buffers)
    return local_call(functools.partial(slot_kernel, slots, inward), len(given), made, name, 1)


def halves_kernel(both, first, second):
    for j in range(first.shape[0]):
        first[j], second[j] = both[j, 0], both[j, 1]


def near_rows(where_ref, side, rows, far):
    bit = where_ref[1] // 2 if side == 0 else where_ref[1] % 2
    return pl.ds(pl.multiple_of((bit ^ far) * rows, 16), rows)


def widen_kernel(where_ref, both, got_first, got_second, first, second):
    rows = got_first.shape[1]
    for side, (got, out) in enumerate(((got_first, first), (got_second, second))):
        for j in range(4):
            out[j, near_rows(where_ref, side, rows, 0), :] = both[j, side]
            out[j, near_rows(where_ref, side, rows, 1), :] = got[j]


def fold_kernel(where_ref, first, got_first, second, got_second, *made):
    rows = made[0].shape[1]
    for side, (keep, got) in enumerate(((first, got_first), (second, got_second))):
        for far in range(2):
            at = near_rows(where_ref, side, rows, far)
            for j in range(4):
                made[2 * side + far][j] = (keep[j, at, :].astype(F32) + got[j, at, :].astype(F32)).astype(BF)


def pair_kernel(first, got_first, second, got_second, out):
    for j in range(first.shape[0]):
        out[j, 0] = (first[j].astype(F32) + got_first[j].astype(F32)).astype(BF)
        out[j, 1] = (second[j].astype(F32) + got_second[j].astype(F32)).astype(BF)


def stack_kernel(*refs):
    for j, ref in enumerate(refs[:-1]):
        refs[-1][j] = ref[...]


def relay_kernel(to_x, to_y, for_y, for_x, out_x, out_y):
    out_x[:2] = to_x[:2]
    out_x[2:] = (to_x[2:].astype(F32) + for_x[...].astype(F32)).astype(BF)
    out_y[:2] = (to_y[:2].astype(F32) + for_y[...].astype(F32)).astype(BF)
    out_y[2:] = to_y[2:]


def split_kernel(own, by_x, by_y, vectors, *made):
    for j, out in enumerate(made):
        columns = own.shape[2]
        out[:, :columns] = (own[j].astype(F32) + by_x[j].astype(F32) + by_y[j].astype(F32)).astype(BF)
        out[:, columns:] = vectors[...]


def row_moves(shards, spans, seqs):
    chips = spans // (2 * seqs)
    moves = ([], [])
    for shard in range(shards):
        for span in range(spans):
            for item in range(seqs):
                sequence = (shard % 2) * seqs + item
                rank = span // seqs
                target = (shard - shard % 2 + rank % 2) * spans + sequence * chips + rank // 2
                moves[(item + span) % 2].append((shard * spans + span, target))
    return moves


def back_moves(moves):
    return tuple([(b, a) for a, b in one] for one in moves)


def group_moves(shards, spans, ranks):
    chips = ranks // 2
    moves = []
    for k in range(1, ranks):
        one = []
        for shard in range(shards):
            for span in range(spans):
                rank = (span % chips) * 2 + shard % 2
                other = rank ^ k
                target = (shard - shard % 2 + other % 2) * spans + span - span % chips + other // 2
                one.append((shard * spans + span, target))
        moves.append(one)
    return moves


def body(
    tokens, weight_qkv, weight_out, weight_in, weight_back, gains_in, shifts_in, biases_in, ff_bias_in, cotangent
):
    seqs, span, width = tokens.shape
    shards, spans = lax.axis_size("shard"), lax.axis_size("ctx")
    shard, ctx = lax.axis_index("shard"), lax.axis_index("ctx")
    ranks = spans // seqs
    rows, length = seqs * span, spans * span
    chips = ranks // 2
    rank = (ctx % chips) * 2 + shard % 2
    core = shard % 2
    hidden = weight_back.shape[0] * shards * spans
    part, ff_part = width // ranks, hidden // ranks
    blocks = shards * spans
    heads = HEADS // ranks
    local = weight_qkv.shape[0]
    lanes = 2 * HEAD_DIM if heads % 2 == 0 else heads * HEAD_DIM
    groups = part // lanes
    scale = HEAD_DIM ** (-0.5)
    moves = row_moves(shards, spans, seqs)
    returns = back_moves(moves)
    turns = group_moves(shards, spans, ranks)
    odd_span = ctx % 2
    odd_sequence = (ctx // chips) % 2
    replicas = lax.axis_size("replica")
    paired = shards == 2 and spans == 4 and replicas == 4 and ranks == 2

    def row_parts(items):
        one = lax.ppermute(lax.dynamic_index_in_dim(items, odd_span, 0, False), LINE, moves[0])
        two = lax.ppermute(lax.dynamic_index_in_dim(items, 1 - odd_span, 0, False), LINE, moves[1])
        return one, two

    def to_rows(one, two):
        return jnp.where(odd_sequence == 0, jnp.concatenate([one, two]), jnp.concatenate([two, one]))

    def from_rows_parts(low):
        items = low.reshape(seqs, span, width)
        one = lax.ppermute(lax.dynamic_index_in_dim(items, odd_sequence, 0, False), LINE, returns[0])
        two = lax.ppermute(lax.dynamic_index_in_dim(items, 1 - odd_sequence, 0, False), LINE, returns[1])
        return one, two

    def from_rows(one, two):
        return jnp.where(odd_span == 0, jnp.stack([one, two]), jnp.stack([two, one]))

    def gather_rows(low):
        return jnp.concatenate([low] + [lax.ppermute(low, LINE, one) for one in turns])

    def scatter_rows(items, product):
        got = []
        for k, one in enumerate(turns):
            sent = product(items[(k + 1) * rows : (k + 2) * rows]).astype(BF)
            got.append(lax.ppermute(sent, LINE, one))
        total = product(items[:rows])
        for one in got:
            total = total + one.astype(F32)
        return total

    def swap(items):
        return lax.ppermute(items, "shard", [(0, 1), (1, 0)])

    def gather_columns(weight):
        whole = lax.all_gather(weight, LINE, axis=0, tiled=True)
        return lax.dynamic_index_in_dim(whole, rank, 1, False)

    def gather_lines(weight):
        whole = lax.all_gather(weight, LINE, axis=0, tiled=True)
        size = whole.shape[0] // ranks
        return lax.dynamic_slice_in_dim(whole, rank * size, size, 0)

    def scatter_columns(grad):
        whole = jnp.zeros((grad.shape[0], ranks, grad.shape[1]), BF)
        whole = lax.dynamic_update_slice_in_dim(whole, grad[:, None], rank, 1)
        owned = lax.psum_scatter(whole, LINE, scatter_dimension=0, tiled=True)
        return lax.psum(owned, "replica").astype(F32)

    def scatter_lines(grad):
        whole = jnp.zeros((grad.shape[0] * ranks, grad.shape[1]), BF)
        whole = lax.dynamic_update_slice_in_dim(whole, grad, rank * grad.shape[0], 0)
        owned = lax.psum_scatter(whole, LINE, scatter_dimension=0, tiled=True)
        return lax.psum(owned, "replica").astype(F32)

    replica = lax.axis_index("replica")
    where = jnp.stack([ctx, replica]).astype(jnp.int32)

    def along_z(items, step):
        return lax.ppermute(items, "ctx", [(i, i ^ step) for i in range(4)])

    def across(items, step):
        return lax.ppermute(items, "replica", [(i, i ^ step) for i in range(4)])

    def after(items, *others):
        return lax.optimization_barrier((items, others))[0] if paired else items

    def z_moves(own):
        return [along_z(own, step) for step in (1, 2, 3)]

    def stacked(own, seen, name):
        return local_call(stack_kernel, 4, [low_shape(4, *own.shape)], name)(own, *seen)[0]

    def xy_moves(four):
        return across(four, 1), across(four, 2)

    def relay_parts(by_x, by_y):
        return by_x[:2], by_y[2:]

    def relays(for_y, for_x):
        return across(for_y, 2), across(for_x, 1)

    def relayed(buffers, got, name):
        shape = low_shape(*buffers[0].shape)
        return local_call(relay_kernel, 4, [shape] * 2, name)(buffers[1], buffers[2], *got)

    def split(own, got, vectors, name):
        shape = low_shape(own.shape[1], own.shape[2] + vectors.shape[1])
        return local_call(split_kernel, 4, [shape] * 4, name)(own, *got, vectors)

    def z_sum(own, got):
        return (own.astype(F32) + got[0].astype(F32) + got[1].astype(F32) + got[2].astype(F32)).astype(BF)

    def plus(a, b):
        return (a.astype(F32) + b.astype(F32)).astype(BF)

    def by_quarters(one, got):
        one, by_x, by_y, by_both = [i.astype(F32) for i in (one, *got)]
        quarters = []
        for quarter in range(4):
            step = replica ^ quarter
            near = jnp.where(step == 0, one, by_x)
            quarters.append(jnp.where(step < 2, near, jnp.where(step == 2, by_y, by_both)))
        return quarters

    bits = (replica % 2, replica // 2)

    def of_core(weight, kinds, one_core):
        size = weight.shape[1] // (kinds * ranks)
        starts = [(kind * ranks + one_core) * size for kind in range(kinds)]
        return jnp.concatenate([lax.dynamic_slice_in_dim(weight, at, size, 1) for at in starts], 1)

    def by_halves(weight, kinds):
        mine, other = of_core(weight, kinds, core), swap(of_core(weight, kinds, 1 - core))
        blocks_of = jnp.where(core == 0, mine, other), jnp.where(core == 0, other, mine)
        return [
            lax.dynamic_slice_in_dim(one, bit * (local // 2), local // 2, 0) for one, bit in zip(blocks_of, bits)
        ]

    def by_quarter(weight, kinds):
        mine, other = of_core(weight, kinds, core), swap(of_core(weight, kinds, 1 - core))
        chosen = jnp.where(core == replica // 2, mine, other)
        return lax.dynamic_slice_in_dim(chosen, (replica % 2) * (local // 2), local // 2, 0)

    def to_shard(first, second):
        mine, other = jnp.where(core == 0, first, second), jnp.where(core == 0, second, first)
        other = swap(other.astype(BF)).astype(F32)
        return jnp.where(core == 0, mine, other), jnp.where(core == 0, other, mine)

    def slot_groups():
        ff_local = weight_back.shape[0]
        half, ff_half, wide = local // 2, ff_local // 2, 3 * part
        third = width // 2

        def attention_pieces(where):
            for buffer, (step, first, count) in enumerate(((0, 0, 4), (1, 0, 4), (2, 0, 4), (3, 0, 2), (3, 2, 2))):
                quarter = where[1] ^ step
                for j in range(count):
                    at = (where[0] ^ (first + j)) * local + (quarter % 2) * half
                    column = pl.multiple_of((quarter // 2) * third, 128)
                    parts = [(1, (0, half), (wide, third), at, (column, third))]
                    for group in range(groups):
                        for kind in range(3):
                            low, high = kind * part + group * lanes, (3 * group + kind) * lanes
                            row = (quarter // 2) * third + at
                            parts.append((0, (0, half), (low, lanes), row, (high, lanes)))
                    yield buffer, (j,), parts

        def ff_parts(side, cut, z):
            at = side * third + z * local + cut * half
            row = z * ff_local + side * ff_half + cut * (ff_half // 2)
            return (
                (0, (0, half), (0, width), at, (0, width)),
                (0, (half, half), (0, width), at, (width, width)),
                (1, (2 * half, ff_half // 2), (0, width), row, (0, width)),
            )

        def ff_pieces(where):
            for side, bit in enumerate((where[1] % 2, where[1] // 2)):
                for z in range(4):
                    yield 2 * side, (z,), ff_parts(side, bit, z)
                    yield 2 * side + 1, (z,), ff_parts(side, 1 - bit, z)

        attention = (half, wide + third)
        feed = (2 * half + ff_half // 2, width)
        shapes = [(width, ff_part), (ff_part, width)]
        return (
            Slots([(width, wide), (part, width)], [(n, *attention) for n in (4, 4, 4, 2, 2)], attention_pieces),
            Slots(shapes, [(4, *feed)] * 4, ff_pieces),
        )

    small_in = jnp.concatenate(
        [gains_in, shifts_in, biases_in, ff_bias_in.reshape(hidden // width, width // blocks)]
    )
    if paired:
        attention_slots, ff_slots = slot_groups()
        half, third = local // 2, width // 2
        small_near = swap(small_in)
        lines = lax.dynamic_slice(weight_out, ((replica % 2) * half, (replica // 2) * third), (half, third))
        own = jnp.concatenate([by_quarter(weight_qkv, 3), lines], 1)
        seen = z_moves(own)
        owns = []
        ff_quarter = weight_back.shape[0] // 4
        for side, one in enumerate(by_halves(weight_in, 1)):
            at = (2 * side + bits[side]) * ff_quarter
            lines = lax.dynamic_slice_in_dim(weight_back, at, ff_quarter, 0)
            owns.append(jnp.where(bits[1 - side] == 0, jnp.concatenate([one[:, :width], one[:, width:]]), lines))
        owns = jnp.stack(owns)
        ff_own = lax.all_gather(owns, "ctx", axis=0)
        seen_small = after(jnp.stack([small_in, small_near]), own)
        seen_small = jnp.concatenate([seen_small] + [along_z(seen_small, step) for step in (1, 2, 3)])
        four = stacked(own, after(seen, (owns, seen_small)), "stack_attention")
        xy = xy_moves(four)
        token_parts = after(row_parts(tokens), four)
        pieces = relay_parts(*xy)
        relay = relays(*pieces)
        qkv_part, out_part = slot_call(attention_slots, True, "join_attention")(where, four, *xy, *relay)
    else:
        ordered = weight_qkv.reshape(local, 3, ranks, groups, lanes).transpose(0, 2, 3, 1, 4)
        qkv_part = gather_columns(ordered.reshape(local, ranks, 3 * part))
        out_part = gather_lines(weight_out)
        in_part = gather_columns(weight_in.reshape(local, ranks, ff_part))
        back_part = gather_lines(weight_back)
        token_parts = row_parts(tokens)

    if paired:
        every = jnp.arange(8)
        near = ctx ^ (every % 4)
        small = jnp.take(seen_small, 2 * near + (core ^ (every // 4)), axis=0).astype(F32)
    else:
        small = lax.all_gather(small_in, LINE, axis=0).astype(F32)
    vectors = small[:, :8].swapaxes(0, 1).reshape(8, width)
    gains, shifts, biases = vectors[0:2], vectors[2:4], vectors[4:8]
    ff_bias = lax.dynamic_slice_in_dim(small[:, 8:].reshape(hidden), rank * ff_part, ff_part, 0)

    def of_rank(vector):
        return lax.dynamic_slice_in_dim(vector, rank * part, part, 0).reshape(groups, lanes)

    none = jnp.zeros((groups, lanes), F32)
    qkv_bias = jnp.stack([of_rank(biases[0]), none, of_rank(biases[1])], 1).reshape(-1)
    qkv_scale = jnp.stack([none + scale, none + 1, none + 1], 1).reshape(-1)
    attend, attend_back = attention_calls(length, rows, groups, lanes)
    rank_word = rank.astype(jnp.int32).reshape(1)

    inputs = to_rows(*token_parts).astype(F32)
    normed_one, spread_one = normalize(inputs)
    first_all = gather_rows((normed_one * gains[0] + shifts[0]).astype(BF))
    if paired:
        quarters = [low_shape(4, *owns.shape[1:])] * 2
        ff_near = local_call(halves_kernel, 1, quarters, "halves_ff")(after(ff_own, qkv_part))
        ff_got = across(ff_near[0], 2), across(ff_near[1], 1)
        first_all = after(first_all, ff_near)
    qkv = ((dot(first_all, qkv_part) + qkv_bias) * qkv_scale).astype(BF)
    mixed, logs = attend(rank_word, qkv)
    if paired:
        halves = [low_shape(4, 2 * owns.shape[1], width)] * 2
        ff_near = local_call(widen_kernel, 3, halves, "widen_ff", 1)(where, ff_own, *after(ff_got, mixed))
        ff_far = across(ff_near[0], 1), across(ff_near[1], 2)
        mixed = after(mixed, ff_near)
        cotangent = after(cotangent, ff_near)
    cotangent_parts = row_parts(cotangent)
    hidden_in = inputs + scatter_rows(mixed, lambda one: dot(one, out_part)) + biases[2]
    normed_two, spread_two = normalize(hidden_in)
    second = (normed_two * gains[1] + shifts[1]).astype(BF)
    second_all = gather_rows(second)
    if paired:
        in_part, back_part = slot_call(ff_slots, True, "join_ff")(
            where, ff_near[0], after(ff_far[0], second), ff_near[1], after(ff_far[1], second)
        )
    inner = dot(second_all, in_part) + ff_bias
    active = jax.nn.gelu(inner).astype(BF)
    grad_low = to_rows(*after(cotangent_parts, active))
    result = hidden_in + scatter_rows(active, lambda one: dot(one, back_part)) + biases[3]
    output_parts = from_rows_parts(result.astype(BF))

    grad_rows = grad_low.astype(F32)
    grad_all = gather_rows(grad_low)
    grad_active = dot_nt(grad_all, back_part)
    grad_inner = jax.vjp(jax.nn.gelu, inner)[1](grad_active)[0].astype(BF)
    grad_back = dot_tn(active, grad_all).astype(BF)
    grad_in = dot_tn(second_all, grad_inner).astype(BF)
    if paired:
        ff_buffers = slot_call(ff_slots, False, "part_ff")(where, grad_in, grad_back)
        ff_got = across(ff_buffers[1], 1), across(ff_buffers[3], 2)
        grad_inner = after(grad_inner, ff_buffers)
    grad_second = scatter_rows(grad_inner, lambda one: dot_nt(one, in_part))
    grad_hidden = grad_rows + norm_back(grad_second * gains[1], normed_two, spread_two)

    grad_branch = grad_hidden.astype(BF)
    branch_all = gather_rows(grad_branch)
    grad_mixed = dot_nt(branch_all, out_part).astype(BF)
    early = (
        jnp.sum(grad_second * normed_two, 0),
        jnp.sum(grad_second, 0),
        jnp.sum(grad_branch.astype(F32), 0),
        jnp.sum(grad_rows, 0),
        jnp.sum(grad_inner.astype(F32), 0),
    )
    if paired:
        ff_got = after(ff_got, early)
        ff_sums = local_call(fold_kernel, 4, quarters * 2, "fold_ff", 1)(
            where, ff_buffers[0], *after((ff_got[0], ff_buffers[2], ff_got[1]), branch_all)
        )
        ff_got = across(ff_sums[1], 2), across(ff_sums[3], 1)
        grad_mixed = after(grad_mixed, ff_sums)
    grad_qkv = attend_back(rank_word, qkv, grad_mixed, logs)
    if paired:
        output_parts = after(output_parts, grad_qkv)
        ff_got = after(ff_got, (grad_qkv, output_parts))
        ff_sums = local_call(pair_kernel, 4, [low_shape(4, 2, *ff_sums[0].shape[1:])], "add_ff")(
            ff_sums[0], ff_got[0], ff_sums[2], ff_got[1]
        )[0]
        grad_qkv = after(grad_qkv, ff_sums)
        ff_one = lax.psum_scatter(
            ff_sums.reshape(-1, width), "ctx", scatter_dimension=0, tiled=True
        ).reshape(ff_sums.shape[1:])
    output = from_rows(*output_parts)
    grad_first = scatter_rows(grad_qkv, lambda one: dot_nt(one, qkv_part))
    grad_out = dot_tn(mixed, branch_all).astype(BF)
    grad_weight = dot_tn(first_all, grad_qkv).astype(BF)
    if paired:
        buffers = slot_call(attention_slots, False, "part_attention")(where, grad_weight, grad_out)
        got = across(buffers[3], 1), across(buffers[4], 2)
        sent = relayed(buffers, got, "relay_attention")
        grad_first, ff_one = after((grad_first, ff_one), sent)
    grad_inputs = grad_hidden + norm_back(grad_first * gains[0], normed_one, spread_one)
    grad_tokens_low = grad_inputs.astype(BF)
    if paired:
        grad_tokens_low = after(grad_tokens_low, sent)
    grad_token_parts = from_rows_parts(grad_tokens_low)

    qkv_sums = jnp.sum(grad_qkv.astype(F32), 0).reshape(groups, 3, lanes)

    def at_rank(vector, size):
        return lax.dynamic_update_slice_in_dim(jnp.zeros((size,), F32), vector, rank * vector.shape[0], 0)

    sums = jnp.stack(
        [
            jnp.sum(grad_first * normed_one, 0),
            early[0],
            jnp.sum(grad_first, 0),
            early[1],
            at_rank(qkv_sums[:, 0].reshape(part), width),
            at_rank(qkv_sums[:, 2].reshape(part), width),
            early[2],
            early[3],
        ]
    )
    ff_sums_of = at_rank(early[4], hidden)
    if paired:
        wide = 3 * part
        got = across(sent[0], 1), across(sent[1], 2)
        vectors = jnp.concatenate([sums.reshape(-1), ff_sums_of.reshape(-1)]).astype(BF)
        lane_block = 128 * (-(-vectors.size // (128 * (local // 2))))
        vectors = jnp.pad(vectors, (0, lane_block * (local // 2) - vectors.size)).reshape(local // 2, lane_block)
        parts = split(buffers[0], got, vectors, "split_attention")
        got = [along_z(parts[step], step) for step in (1, 2, 3)]
        ff_got = across(ff_one[0], 2), across(ff_one[1], 1)
        ff_halves = []
        for bit, mine, other in zip(bits[::-1], ff_one, ff_got):
            ff_halves.append(jnp.where(bit == 0, jnp.concatenate([mine, other]), jnp.concatenate([other, mine])))
        ff_got = across(ff_halves[0], 1), across(ff_halves[1], 2)
        ff_owned = []
        for bit, mine, other in zip(bits, ff_halves, ff_got):
            mine, other = mine.astype(F32), other.astype(F32)
            ff_owned.append((jnp.where(bit == 0, mine, other), jnp.where(bit == 0, other, mine)))
        grad_token_parts = after(grad_token_parts, parts)
        one = z_sum(parts[0], after(got, grad_token_parts))
        grad_token_parts = after(grad_token_parts, one)
        quarters = by_quarters(one, [across(one, step) for step in (1, 2, 3)])
        vectors = [i[:, wide + third :] for i in quarters]
        vectors = vectors[0] + vectors[1] + vectors[2] + vectors[3]
        joined = [jnp.concatenate(quarters[:2]), jnp.concatenate(quarters[2:])]
        owned_out = jnp.concatenate([one[:, wide : wide + third] for one in joined], 1)
        low, high = to_shard(*[one[:, :wide] for one in joined])
        owned_qkv = [i[:, kind * part : (kind + 1) * part] for kind in range(3) for i in (low, high)]
        owned_qkv = jnp.concatenate(owned_qkv, 1)
        half = local // 2
        blocks_in = [
            jnp.concatenate([jnp.concatenate([cut[:half], cut[half : 2 * half]], 1) for cut in one]) for one in ff_owned
        ]
        owned_in = jnp.concatenate(to_shard(*blocks_in), 1)
        owned_back = jnp.concatenate([cut[2 * half :] for one in ff_owned for cut in one])
    else:
        owned_back, owned_in = scatter_lines(grad_back), scatter_columns(grad_in).reshape(local, hidden)
        owned_out, owned_qkv = scatter_lines(grad_out), scatter_columns(grad_weight)
        owned_qkv = owned_qkv.reshape(local, ranks, groups, 3, lanes)
        owned_qkv = owned_qkv.transpose(0, 3, 1, 2, 4).reshape(local, 3 * width)

    if paired:
        total = (vectors + swap(vectors)).reshape(-1)
        sums, ff_sums_of = total[: 8 * width].reshape(8, width), total[8 * width : 8 * width + hidden]
    else:
        sums, ff_sums_of = lax.psum((sums, ff_sums_of), EVERY)
    grad_tokens = from_rows(*grad_token_parts)
    at = shard * spans + ctx
    mine = lax.dynamic_slice_in_dim(sums, at * (width // blocks), width // blocks, 1)
    ff_mine = lax.dynamic_slice_in_dim(ff_sums_of, at * (hidden // blocks), hidden // blocks, 0)
    return (
        output,
        grad_tokens,
        owned_qkv,
        owned_out,
        owned_in,
        owned_back,
        mine[0:2],
        mine[2:4],
        mine[4:8],
        ff_mine,
    )


def solution(mesh):
    rows = P(("replica", "shard"), "ctx", None)
    lines, columns, flat = P(LINE, None), P(None, LINE), P(LINE)
    return jax.shard_map(
        body,
        mesh=mesh,
        in_specs=(rows, lines, lines, lines, lines, columns, columns, columns, flat, rows),
        out_specs=(rows, rows, lines, lines, lines, lines, columns, columns, columns, flat),
        check_vma=False,
    )
```

```python
import functools

import jax
import jax.numpy as jnp
from jax import lax
from jax.experimental import pallas as pl
from jax.experimental.pallas import tpu as pltpu
from jax.sharding import PartitionSpec as P

HEADS = 12
HEAD_DIM = 64
EPS = 1e-05
NEG = -1e30
BLOCK = 256
LINE = ("shard", "ctx")
EVERY = ("replica", "shard", "ctx")
BF = jnp.bfloat16
F32 = jnp.float32


def normalize(values):
    centered = values - jnp.mean(values, -1, keepdims=True)
    spread = lax.rsqrt(jnp.mean(centered * centered, -1, keepdims=True) + EPS)
    return centered * spread, spread


def norm_back(upstream, normed, spread):
    first_mean = jnp.mean(upstream, -1, keepdims=True)
    second_mean = jnp.mean(upstream * normed, -1, keepdims=True)
    return spread * (upstream - first_mean - normed * second_mean)


def dot(a, b):
    return jnp.dot(a, b, preferred_element_type=F32)


def dot_nt(a, b):
    return lax.dot_general(a, b, (((1,), (1,)), ((), ())), preferred_element_type=F32)


def dot_tn(a, b):
    return lax.dot_general(a, b, (((0,), (0,)), ((), ())), preferred_element_type=F32)


def place(rank, block, rows):
    per_rank = rows // BLOCK
    owner, part = block // per_rank, block % per_rank
    return pl.multiple_of((owner ^ rank) * rows + part * BLOCK, BLOCK)


def head_mask(lanes, head):
    lane = lax.broadcasted_iota(jnp.int32, (BLOCK, lanes), 1)
    return (lane >= head * HEAD_DIM) & (lane < (head + 1) * HEAD_DIM)


def diagonal(scores):
    key = lax.broadcasted_iota(jnp.int32, scores.shape, 0)
    query = lax.broadcasted_iota(jnp.int32, scores.shape, 1)
    return jnp.where(key <= query, scores, NEG)


def attend_kernel(rows, rank_ref, qkv_ref, mixed_ref, log_ref, keys, values_t):
    length, lanes = mixed_ref.shape
    rank = rank_ref[0]
    heads = lanes // HEAD_DIM
    for block in range(length // BLOCK):
        at = pl.ds(place(rank, block, rows), BLOCK)
        here = slice(block * BLOCK, (block + 1) * BLOCK)
        keys[here, :] = qkv_ref[at, lanes : 2 * lanes]
        values_t[:, here] = qkv_ref[at, 2 * lanes :].T
    for block in range(length // BLOCK):
        at = pl.ds(place(rank, block, rows), BLOCK)
        start, stop = block * BLOCK, (block + 1) * BLOCK
        query = qkv_ref[at, :lanes]
        parts = []
        for head in range(heads):
            one = slice(head * HEAD_DIM, (head + 1) * HEAD_DIM)
            one_query = jnp.where(head_mask(lanes, head), query, jnp.zeros_like(query))
            near = diagonal(dot_nt(keys[start:stop, :], one_query))
            highest = jnp.max(near, 0, keepdims=True)
            if block:
                far = dot_nt(keys[:start, :], one_query)
                highest = jnp.maximum(highest, jnp.max(far, 0, keepdims=True))
            near = jnp.exp(near - highest)
            total = jnp.sum(near, 0, keepdims=True)
            mixed = dot(values_t[one, start:stop], near.astype(BF))
            if block:
                far = jnp.exp(far - highest)
                total = total + jnp.sum(far, 0, keepdims=True)
                mixed = mixed + dot(values_t[one, :start], far.astype(BF))
            parts.append(mixed / total)
            log_ref[head : head + 1, start:stop] = highest + jnp.log(total)
        mixed_ref[at, :] = jnp.concatenate(parts, 0).T.astype(BF)


def attend_back_kernel(
    rows, rank_ref, qkv_ref, grad_ref, log_ref, out_ref, keys, values, keys_t, key_sum, value_sum
):
    length, lanes = grad_ref.shape
    rank = rank_ref[0]
    heads = lanes // HEAD_DIM
    scale = HEAD_DIM ** (-0.5)
    for block in range(length // BLOCK):
        at = pl.ds(place(rank, block, rows), BLOCK)
        here = slice(block * BLOCK, (block + 1) * BLOCK)
        key = qkv_ref[at, lanes : 2 * lanes]
        keys[here, :] = key
        keys_t[:, here] = key.T
        values[here, :] = qkv_ref[at, 2 * lanes :]
    for block in range(length // BLOCK):
        at = pl.ds(place(rank, block, rows), BLOCK)
        start, stop = block * BLOCK, (block + 1) * BLOCK
        query = qkv_ref[at, :lanes]
        grad = grad_ref[at, :]
        parts = []
        near_key = near_value = far_key = far_value = None
        for head in range(heads):
            one = slice(head * HEAD_DIM, (head + 1) * HEAD_DIM)
            mask = head_mask(lanes, head)
            one_query = jnp.where(mask, query, jnp.zeros_like(query))
            one_grad = jnp.where(mask, grad, jnp.zeros_like(grad))
            logs = log_ref[head : head + 1, start:stop]
            near = jnp.exp(diagonal(dot_nt(keys[start:stop, :], one_query)) - logs)
            near_grad = dot_nt(values[start:stop, :], one_grad)
            level = jnp.sum(near * near_grad, 0, keepdims=True)
            if block:
                far = jnp.exp(dot_nt(keys[:start, :], one_query) - logs)
                far_grad = dot_nt(values[:start, :], one_grad)
                level = level + jnp.sum(far * far_grad, 0, keepdims=True)
            near_low = near.astype(BF)
            near_scores = (near * (near_grad - level)).astype(BF)
            value_term, key_term = dot(near_low, one_grad), dot(near_scores, one_query)
            near_value = value_term if near_value is None else near_value + value_term
            near_key = key_term if near_key is None else near_key + key_term
            query_term = dot(keys_t[one, start:stop], near_scores)
            if block:
                far_low = far.astype(BF)
                far_scores = (far * (far_grad - level)).astype(BF)
                value_term, key_term = dot(far_low, one_grad), dot(far_scores, one_query)
                far_value = value_term if far_value is None else far_value + value_term
                far_key = key_term if far_key is None else far_key + key_term
                query_term = query_term + dot(keys_t[one, :start], far_scores)
            parts.append(query_term)
        key_sum[start:stop, :] = near_key
        value_sum[start:stop, :] = near_value
        if block:
            key_sum[:start, :] += far_key
            value_sum[:start, :] += far_value
        query_grad = jnp.concatenate(parts, 0).T.astype(BF).astype(F32) * scale
        out_ref[at, :lanes] = query_grad.astype(BF)
    for block in range(length // BLOCK):
        at = pl.ds(place(rank, block, rows), BLOCK)
        here = slice(block * BLOCK, (block + 1) * BLOCK)
        out_ref[at, lanes : 2 * lanes] = key_sum[here, :].astype(BF)
        out_ref[at, 2 * lanes :] = value_sum[here, :].astype(BF)


def attention_calls(length, rows, groups, lanes):
    heads = lanes // HEAD_DIM
    wide = pl.BlockSpec((length, 3 * lanes), lambda g, r: (0, g))
    thin = pl.BlockSpec((length, lanes), lambda g, r: (0, g))
    logs = pl.BlockSpec((None, heads, length), lambda g, r: (g, 0, 0))
    pairs = groups * heads * length * length // 2
    params = pltpu.CompilerParams(vmem_limit_bytes=56 * 2**20)
    forward = pl.pallas_call(
        functools.partial(attend_kernel, rows),
        grid_spec=pltpu.PrefetchScalarGridSpec(
            num_scalar_prefetch=1,
            grid=(groups,),
            in_specs=[wide],
            out_specs=[thin, logs],
            scratch_shapes=[pltpu.VMEM((length, lanes), BF), pltpu.VMEM((lanes, length), BF)],
        ),
        out_shape=[
            jax.ShapeDtypeStruct((length, groups * lanes), BF),
            jax.ShapeDtypeStruct((groups, heads, length), F32),
        ],
        cost_estimate=pl.CostEstimate(
            flops=pairs * 16 * HEAD_DIM, bytes_accessed=length * groups * lanes * 8, transcendentals=pairs
        ),
        compiler_params=params,
        name="attend",
    )
    backward = pl.pallas_call(
        functools.partial(attend_back_kernel, rows),
        grid_spec=pltpu.PrefetchScalarGridSpec(
            num_scalar_prefetch=1,
            grid=(groups,),
            in_specs=[wide, thin, logs],
            out_specs=wide,
            scratch_shapes=[
                pltpu.VMEM((length, lanes), BF),
                pltpu.VMEM((length, lanes), BF),
                pltpu.VMEM((lanes, length), BF),
                pltpu.VMEM((length, lanes), F32),
                pltpu.VMEM((length, lanes), F32),
            ],
        ),
        out_shape=jax.ShapeDtypeStruct((length, 3 * groups * lanes), BF),
        cost_estimate=pl.CostEstimate(
            flops=pairs * 40 * HEAD_DIM, bytes_accessed=length * groups * lanes * 14, transcendentals=pairs
        ),
        compiler_params=params,
        name="attend_back",
    )
    return forward, backward


class Slots:
    def __init__(self, shapes, buffers, pieces):
        self.shapes, self.buffers, self.pieces = shapes, buffers, pieces

    def copies(self, where, buffers, arrays, move):
        for buffer, index, parts in self.pieces(where):
            for array, slot_rows, slot_columns, row, columns in parts:
                one = buffers[buffer].at[(*index, pl.ds(*slot_rows), pl.ds(*slot_columns))]
                two = arrays[array].at[pl.ds(pl.multiple_of(row, 16), slot_rows[1]), pl.ds(*columns)]
                move(one, two)


def slot_kernel(slots, inward, where_ref, *refs):
    size = len(slots.buffers) if inward else len(slots.shapes)
    arrays, buffers = (refs[size:], refs[:size]) if inward else (refs[:size], refs[size:])

    def move(low, high):
        source, target = (low, high) if inward else (high, low)
        target[...] = source[...]

    slots.copies([where_ref[i] for i in range(2)], buffers, arrays, move)


def local_call(kernel, given, made, name, scalars=0):
    size = 2 * sum(2 * one.size for one in made)
    specs = [pl.BlockSpec(memory_space=pltpu.SMEM)] * scalars
    return pl.pallas_call(
        kernel,
        in_specs=specs + [pl.BlockSpec(memory_space=pltpu.VMEM)] * given,
        out_specs=[pl.BlockSpec(memory_space=pltpu.VMEM)] * len(made),
        out_shape=made,
        compiler_params=pltpu.CompilerParams(vmem_limit_bytes=40 * 2**20),
        cost_estimate=pl.CostEstimate(flops=0, bytes_accessed=size, transcendentals=0),
        name=name,
    )


def low_shape(*shape):
    return jax.ShapeDtypeStruct(shape, BF)


def slot_call(slots, inward, name):
    arrays = [low_shape(*shape) for shape in slots.shapes]
    buffers = [low_shape(*shape) for shape in slots.buffers]
    given, made = (buffers, arrays) if inward else (arrays, buffers)
    return local_call(functools.partial(slot_kernel, slots, inward), len(given), made, name, 1)


def halves_kernel(both, first, second):
    for j in range(first.shape[0]):
        first[j], second[j] = both[j, 0], both[j, 1]


def near_rows(where_ref, side, rows, far):
    bit = where_ref[1] // 2 if side == 0 else where_ref[1] % 2
    return pl.ds(pl.multiple_of((bit ^ far) * rows, 16), rows)


def widen_kernel(where_ref, both, got_first, got_second, first, second):
    rows = got_first.shape[1]
    for side, (got, out) in enumerate(((got_first, first), (got_second, second))):
        for j in range(4):
            out[j, near_rows(where_ref, side, rows, 0), :] = both[j, side]
            out[j, near_rows(where_ref, side, rows, 1), :] = got[j]


def fold_kernel(where_ref, first, got_first, second, got_second, *made):
    rows = made[0].shape[1]
    for side, (keep, got) in enumerate(((first, got_first), (second, got_second))):
        for far in range(2):
            at = near_rows(where_ref, side, rows, far)
            for j in range(4):
                made[2 * side + far][j] = (keep[j, at, :].astype(F32) + got[j, at, :].astype(F32)).astype(BF)


def pair_kernel(first, got_first, second, got_second, out):
    for j in range(first.shape[0]):
        out[j, 0] = (first[j].astype(F32) + got_first[j].astype(F32)).astype(BF)
        out[j, 1] = (second[j].astype(F32) + got_second[j].astype(F32)).astype(BF)


def stack_kernel(*refs):
    for j, ref in enumerate(refs[:-1]):
        refs[-1][j] = ref[...]


def relay_kernel(to_x, to_y, for_y, for_x, out_x, out_y):
    out_x[:2] = to_x[:2]
    out_x[2:] = (to_x[2:].astype(F32) + for_x[...].astype(F32)).astype(BF)
    out_y[:2] = (to_y[:2].astype(F32) + for_y[...].astype(F32)).astype(BF)
    out_y[2:] = to_y[2:]


def split_kernel(own, by_x, by_y, vectors, *made):
    for j, out in enumerate(made):
        columns = own.shape[2]
        out[:, :columns] = (own[j].astype(F32) + by_x[j].astype(F32) + by_y[j].astype(F32)).astype(BF)
        out[:, columns:] = vectors[...]


def row_moves(shards, spans, seqs):
    chips = spans // (2 * seqs)
    moves = ([], [])
    for shard in range(shards):
        for span in range(spans):
            for item in range(seqs):
                sequence = (shard % 2) * seqs + item
                rank = span // seqs
                target = (shard - shard % 2 + rank % 2) * spans + sequence * chips + rank // 2
                moves[(item + span) % 2].append((shard * spans + span, target))
    return moves


def back_moves(moves):
    return tuple([(b, a) for a, b in one] for one in moves)


def group_moves(shards, spans, ranks):
    chips = ranks // 2
    moves = []
    for k in range(1, ranks):
        one = []
        for shard in range(shards):
            for span in range(spans):
                rank = (span % chips) * 2 + shard % 2
                other = rank ^ k
                target = (shard - shard % 2 + other % 2) * spans + span - span % chips + other // 2
                one.append((shard * spans + span, target))
        moves.append(one)
    return moves


def body(
    tokens, weight_qkv, weight_out, weight_in, weight_back, gains_in, shifts_in, biases_in, ff_bias_in, cotangent
):
    seqs, span, width = tokens.shape
    shards, spans = lax.axis_size("shard"), lax.axis_size("ctx")
    shard, ctx = lax.axis_index("shard"), lax.axis_index("ctx")
    ranks = spans // seqs
    rows, length = seqs * span, spans * span
    chips = ranks // 2
    rank = (ctx % chips) * 2 + shard % 2
    core = shard % 2
    hidden = weight_back.shape[0] * shards * spans
    part, ff_part = width // ranks, hidden // ranks
    blocks = shards * spans
    heads = HEADS // ranks
    local = weight_qkv.shape[0]
    lanes = 2 * HEAD_DIM if heads % 2 == 0 else heads * HEAD_DIM
    groups = part // lanes
    scale = HEAD_DIM ** (-0.5)
    moves = row_moves(shards, spans, seqs)
    returns = back_moves(moves)
    turns = group_moves(shards, spans, ranks)
    odd_span = ctx % 2
    odd_sequence = (ctx // chips) % 2
    replicas = lax.axis_size("replica")
    paired = shards == 2 and spans == 4 and replicas == 4 and ranks == 2

    def row_parts(items):
        one = lax.ppermute(lax.dynamic_index_in_dim(items, odd_span, 0, False), LINE, moves[0])
        two = lax.ppermute(lax.dynamic_index_in_dim(items, 1 - odd_span, 0, False), LINE, moves[1])
        return one, two

    def to_rows(one, two):
        return jnp.where(odd_sequence == 0, jnp.concatenate([one, two]), jnp.concatenate([two, one]))

    def from_rows_parts(low):
        items = low.reshape(seqs, span, width)
        one = lax.ppermute(lax.dynamic_index_in_dim(items, odd_sequence, 0, False), LINE, returns[0])
        two = lax.ppermute(lax.dynamic_index_in_dim(items, 1 - odd_sequence, 0, False), LINE, returns[1])
        return one, two

    def from_rows(one, two):
        return jnp.where(odd_span == 0, jnp.stack([one, two]), jnp.stack([two, one]))

    def gather_rows(low):
        return jnp.concatenate([low] + [lax.ppermute(low, LINE, one) for one in turns])

    def scatter_rows(items, product):
        got = []
        for k, one in enumerate(turns):
            sent = product(items[(k + 1) * rows : (k + 2) * rows]).astype(BF)
            got.append(lax.ppermute(sent, LINE, one))
        total = product(items[:rows])
        for one in got:
            total = total + one.astype(F32)
        return total

    def swap(items):
        return lax.ppermute(items, "shard", [(0, 1), (1, 0)])

    def gather_columns(weight):
        whole = lax.all_gather(weight, LINE, axis=0, tiled=True)
        return lax.dynamic_index_in_dim(whole, rank, 1, False)

    def gather_lines(weight):
        whole = lax.all_gather(weight, LINE, axis=0, tiled=True)
        size = whole.shape[0] // ranks
        return lax.dynamic_slice_in_dim(whole, rank * size, size, 0)

    def scatter_columns(grad):
        whole = jnp.zeros((grad.shape[0], ranks, grad.shape[1]), BF)
        whole = lax.dynamic_update_slice_in_dim(whole, grad[:, None], rank, 1)
        owned = lax.psum_scatter(whole, LINE, scatter_dimension=0, tiled=True)
        return lax.psum(owned, "replica").astype(F32)

    def scatter_lines(grad):
        whole = jnp.zeros((grad.shape[0] * ranks, grad.shape[1]), BF)
        whole = lax.dynamic_update_slice_in_dim(whole, grad, rank * grad.shape[0], 0)
        owned = lax.psum_scatter(whole, LINE, scatter_dimension=0, tiled=True)
        return lax.psum(owned, "replica").astype(F32)

    replica = lax.axis_index("replica")
    where = jnp.stack([ctx, replica]).astype(jnp.int32)

    def along_z(items, step):
        return lax.ppermute(items, "ctx", [(i, i ^ step) for i in range(4)])

    def across(items, step):
        return lax.ppermute(items, "replica", [(i, i ^ step) for i in range(4)])

    def after(items, *others):
        return lax.optimization_barrier((items, others))[0] if paired else items

    def z_moves(own):
        return [along_z(own, step) for step in (1, 2, 3)]

    def stacked(own, seen, name):
        return local_call(stack_kernel, 4, [low_shape(4, *own.shape)], name)(own, *seen)[0]

    def xy_moves(four):
        return across(four, 1), across(four, 2)

    def relay_parts(by_x, by_y):
        return by_x[:2], by_y[2:]

    def relays(for_y, for_x):
        return across(for_y, 2), across(for_x, 1)

    def relayed(buffers, got, name):
        shape = low_shape(*buffers[0].shape)
        return local_call(relay_kernel, 4, [shape] * 2, name)(buffers[1], buffers[2], *got)

    def split(own, got, vectors, name):
        shape = low_shape(own.shape[1], own.shape[2] + vectors.shape[1])
        return local_call(split_kernel, 4, [shape] * 4, name)(own, *got, vectors)

    def z_sum(own, got):
        return (own.astype(F32) + got[0].astype(F32) + got[1].astype(F32) + got[2].astype(F32)).astype(BF)

    def plus(a, b):
        return (a.astype(F32) + b.astype(F32)).astype(BF)

    def by_quarters(one, got):
        one, by_x, by_y, by_both = [i.astype(F32) for i in (one, *got)]
        quarters = []
        for quarter in range(4):
            step = replica ^ quarter
            near = jnp.where(step == 0, one, by_x)
            quarters.append(jnp.where(step < 2, near, jnp.where(step == 2, by_y, by_both)))
        return quarters

    bits = (replica % 2, replica // 2)

    def of_core(weight, kinds, one_core):
        size = weight.shape[1] // (kinds * ranks)
        starts = [(kind * ranks + one_core) * size for kind in range(kinds)]
        return jnp.concatenate([lax.dynamic_slice_in_dim(weight, at, size, 1) for at in starts], 1)

    def by_halves(weight, kinds):
        mine, other = of_core(weight, kinds, core), swap(of_core(weight, kinds, 1 - core))
        blocks_of = jnp.where(core == 0, mine, other), jnp.where(core == 0, other, mine)
        return [
            lax.dynamic_slice_in_dim(one, bit * (local // 2), local // 2, 0) for one, bit in zip(blocks_of, bits)
        ]

    def by_quarter(weight, kinds):
        mine, other = of_core(weight, kinds, core), swap(of_core(weight, kinds, 1 - core))
        chosen = jnp.where(core == replica // 2, mine, other)
        return lax.dynamic_slice_in_dim(chosen, (replica % 2) * (local // 2), local // 2, 0)

    def to_shard(first, second):
        mine, other = jnp.where(core == 0, first, second), jnp.where(core == 0, second, first)
        other = swap(other.astype(BF)).astype(F32)
        return jnp.where(core == 0, mine, other), jnp.where(core == 0, other, mine)

    def slot_groups():
        ff_local = weight_back.shape[0]
        half, ff_half, wide = local // 2, ff_local // 2, 3 * part
        third = width // 2

        def attention_pieces(where):
            for buffer, (step, first, count) in enumerate(((0, 0, 4), (1, 0, 4), (2, 0, 4), (3, 0, 2), (3, 2, 2))):
                quarter = where[1] ^ step
                for j in range(count):
                    at = (where[0] ^ (first + j)) * local + (quarter % 2) * half
                    column = pl.multiple_of((quarter // 2) * third, 128)
                    parts = [(1, (0, half), (wide, third), at, (column, third))]
                    for group in range(groups):
                        for kind in range(3):
                            low, high = kind * part + group * lanes, (3 * group + kind) * lanes
                            row = (quarter // 2) * third + at
                            parts.append((0, (0, half), (low, lanes), row, (high, lanes)))
                    yield buffer, (j,), parts

        def ff_parts(side, cut, z):
            at = side * third + z * local + cut * half
            row = z * ff_local + side * ff_half + cut * (ff_half // 2)
            return (
                (0, (0, half), (0, width), at, (0, width)),
                (0, (half, half), (0, width), at, (width, width)),
                (1, (2 * half, ff_half // 2), (0, width), row, (0, width)),
            )

        def ff_pieces(where):
            for side, bit in enumerate((where[1] % 2, where[1] // 2)):
                for z in range(4):
                    yield 2 * side, (z,), ff_parts(side, bit, z)
                    yield 2 * side + 1, (z,), ff_parts(side, 1 - bit, z)

        attention = (half, wide + third)
        feed = (2 * half + ff_half // 2, width)
        shapes = [(width, ff_part), (ff_part, width)]
        return (
            Slots([(width, wide), (part, width)], [(n, *attention) for n in (4, 4, 4, 2, 2)], attention_pieces),
            Slots(shapes, [(4, *feed)] * 4, ff_pieces),
        )

    small_in = jnp.concatenate(
        [gains_in, shifts_in, biases_in, ff_bias_in.reshape(hidden // width, width // blocks)]
    )
    if paired:
        attention_slots, ff_slots = slot_groups()
        half, third = local // 2, width // 2
        small_near = swap(small_in)
        lines = lax.dynamic_slice(weight_out, ((replica % 2) * half, (replica // 2) * third), (half, third))
        own = jnp.concatenate([by_quarter(weight_qkv, 3), lines], 1)
        seen = z_moves(own)
        owns = []
        ff_quarter = weight_back.shape[0] // 4
        for side, one in enumerate(by_halves(weight_in, 1)):
            at = (2 * side + bits[side]) * ff_quarter
            lines = lax.dynamic_slice_in_dim(weight_back, at, ff_quarter, 0)
            owns.append(jnp.where(bits[1 - side] == 0, jnp.concatenate([one[:, :width], one[:, width:]]), lines))
        owns = jnp.stack(owns)
        ff_own = lax.all_gather(owns, "ctx", axis=0)
        seen_small = after(jnp.stack([small_in, small_near]), own)
        seen_small = jnp.concatenate([seen_small] + [along_z(seen_small, step) for step in (1, 2, 3)])
        four = stacked(own, after(seen, (owns, seen_small)), "stack_attention")
        xy = xy_moves(four)
        token_parts = row_parts(after(tokens, four))
        pieces = relay_parts(*xy)
        relay = relays(*pieces)
        qkv_part, out_part = slot_call(attention_slots, True, "join_attention")(where, four, *xy, *relay)
    else:
        ordered = weight_qkv.reshape(local, 3, ranks, groups, lanes).transpose(0, 2, 3, 1, 4)
        qkv_part = gather_columns(ordered.reshape(local, ranks, 3 * part))
        out_part = gather_lines(weight_out)
        in_part = gather_columns(weight_in.reshape(local, ranks, ff_part))
        back_part = gather_lines(weight_back)
        token_parts = row_parts(tokens)

    if paired:
        every = jnp.arange(8)
        near = ctx ^ (every % 4)
        small = jnp.take(seen_small, 2 * near + (core ^ (every // 4)), axis=0).astype(F32)
    else:
        small = lax.all_gather(small_in, LINE, axis=0).astype(F32)
    vectors = small[:, :8].swapaxes(0, 1).reshape(8, width)
    gains, shifts, biases = vectors[0:2], vectors[2:4], vectors[4:8]
    ff_bias = lax.dynamic_slice_in_dim(small[:, 8:].reshape(hidden), rank * ff_part, ff_part, 0)

    def of_rank(vector):
        return lax.dynamic_slice_in_dim(vector, rank * part, part, 0).reshape(groups, lanes)

    none = jnp.zeros((groups, lanes), F32)
    qkv_bias = jnp.stack([of_rank(biases[0]), none, of_rank(biases[1])], 1).reshape(-1)
    qkv_scale = jnp.stack([none + scale, none + 1, none + 1], 1).reshape(-1)
    attend, attend_back = attention_calls(length, rows, groups, lanes)
    rank_word = rank.astype(jnp.int32).reshape(1)

    inputs = to_rows(*token_parts).astype(F32)
    normed_one, spread_one = normalize(inputs)
    first_all = gather_rows((normed_one * gains[0] + shifts[0]).astype(BF))
    qkv = ((dot(first_all, qkv_part) + qkv_bias) * qkv_scale).astype(BF)
    if paired:
        quarters = [low_shape(4, *owns.shape[1:])] * 2
        ff_near = local_call(halves_kernel, 1, quarters, "halves_ff")(after(ff_own, qkv))
        ff_got = across(ff_near[0], 2), across(ff_near[1], 1)
        qkv = after(qkv, ff_near)
    mixed, logs = attend(rank_word, qkv)
    if paired:
        halves = [low_shape(4, 2 * owns.shape[1], width)] * 2
        ff_near = local_call(widen_kernel, 3, halves, "widen_ff", 1)(where, ff_own, *after(ff_got, mixed))
        ff_far = across(ff_near[0], 1), across(ff_near[1], 2)
        mixed = after(mixed, ff_near)
        cotangent = after(cotangent, ff_near)
    cotangent_parts = row_parts(cotangent)
    hidden_in = inputs + scatter_rows(mixed, lambda one: dot(one, out_part)) + biases[2]
    normed_two, spread_two = normalize(hidden_in)
    second = (normed_two * gains[1] + shifts[1]).astype(BF)
    second_all = gather_rows(second)
    if paired:
        in_part, back_part = slot_call(ff_slots, True, "join_ff")(
            where, ff_near[0], after(ff_far[0], second), ff_near[1], after(ff_far[1], second)
        )
    inner = dot(second_all, in_part) + ff_bias
    active = jax.nn.gelu(inner).astype(BF)
    grad_low = to_rows(*after(cotangent_parts, active))
    result = hidden_in + scatter_rows(active, lambda one: dot(one, back_part)) + biases[3]
    output_parts = from_rows_parts(result.astype(BF))

    grad_rows = grad_low.astype(F32)
    grad_all = gather_rows(grad_low)
    grad_active = dot_nt(grad_all, back_part)
    grad_inner = jax.vjp(jax.nn.gelu, inner)[1](grad_active)[0].astype(BF)
    grad_back = dot_tn(active, grad_all).astype(BF)
    grad_in = dot_tn(second_all, grad_inner).astype(BF)
    if paired:
        ff_buffers = slot_call(ff_slots, False, "part_ff")(where, grad_in, grad_back)
        ff_got = across(ff_buffers[1], 1), across(ff_buffers[3], 2)
        grad_inner = after(grad_inner, ff_buffers)
    grad_second = scatter_rows(grad_inner, lambda one: dot_nt(one, in_part))
    grad_hidden = grad_rows + norm_back(grad_second * gains[1], normed_two, spread_two)

    grad_branch = grad_hidden.astype(BF)
    branch_all = gather_rows(grad_branch)
    grad_mixed = dot_nt(branch_all, out_part).astype(BF)
    early = (
        jnp.sum(grad_second * normed_two, 0),
        jnp.sum(grad_second, 0),
        jnp.sum(grad_branch.astype(F32), 0),
        jnp.sum(grad_rows, 0),
        jnp.sum(grad_inner.astype(F32), 0),
    )
    if paired:
        ff_got = after(ff_got, early)
        ff_sums = local_call(fold_kernel, 4, quarters * 2, "fold_ff", 1)(
            where, ff_buffers[0], *after((ff_got[0], ff_buffers[2], ff_got[1]), branch_all)
        )
        ff_got = across(ff_sums[1], 2), across(ff_sums[3], 1)
        grad_mixed = after(grad_mixed, ff_sums)
    grad_qkv = attend_back(rank_word, qkv, grad_mixed, logs)
    if paired:
        output_parts = after(output_parts, grad_qkv)
        ff_got = after(ff_got, (grad_qkv, output_parts))
        ff_sums = local_call(pair_kernel, 4, [low_shape(4, 2, *ff_sums[0].shape[1:])], "add_ff")(
            ff_sums[0], ff_got[0], ff_sums[2], ff_got[1]
        )[0]
        grad_qkv = after(grad_qkv, ff_sums)
        ff_one = lax.psum_scatter(
            ff_sums.reshape(-1, width), "ctx", scatter_dimension=0, tiled=True
        ).reshape(ff_sums.shape[1:])
    output = from_rows(*output_parts)
    grad_first = scatter_rows(grad_qkv, lambda one: dot_nt(one, qkv_part))
    grad_out = dot_tn(mixed, branch_all).astype(BF)
    grad_weight = dot_tn(first_all, grad_qkv).astype(BF)
    if paired:
        buffers = slot_call(attention_slots, False, "part_attention")(where, grad_weight, grad_out)
        got = across(buffers[3], 1), across(buffers[4], 2)
        sent = relayed(buffers, got, "relay_attention")
        grad_first, ff_one = after((grad_first, ff_one), sent)
    grad_inputs = grad_hidden + norm_back(grad_first * gains[0], normed_one, spread_one)
    grad_tokens_low = grad_inputs.astype(BF)
    if paired:
        grad_tokens_low = after(grad_tokens_low, sent)
    grad_token_parts = from_rows_parts(grad_tokens_low)

    qkv_sums = jnp.sum(grad_qkv.astype(F32), 0).reshape(groups, 3, lanes)

    def at_rank(vector, size):
        return lax.dynamic_update_slice_in_dim(jnp.zeros((size,), F32), vector, rank * vector.shape[0], 0)

    sums = jnp.stack(
        [
            jnp.sum(grad_first * normed_one, 0),
            early[0],
            jnp.sum(grad_first, 0),
            early[1],
            at_rank(qkv_sums[:, 0].reshape(part), width),
            at_rank(qkv_sums[:, 2].reshape(part), width),
            early[2],
            early[3],
        ]
    )
    ff_sums_of = at_rank(early[4], hidden)
    if paired:
        wide = 3 * part
        got = across(sent[0], 1), across(sent[1], 2)
        vectors = jnp.concatenate([sums.reshape(-1), ff_sums_of.reshape(-1)]).astype(BF)
        lane_block = 128 * (-(-vectors.size // (128 * (local // 2))))
        vectors = jnp.pad(vectors, (0, lane_block * (local // 2) - vectors.size)).reshape(local // 2, lane_block)
        parts = split(buffers[0], got, vectors, "split_attention")
        got = [along_z(parts[step], step) for step in (1, 2, 3)]
        ff_got = across(ff_one[0], 2), across(ff_one[1], 1)
        ff_halves = []
        for bit, mine, other in zip(bits[::-1], ff_one, ff_got):
            ff_halves.append(jnp.where(bit == 0, jnp.concatenate([mine, other]), jnp.concatenate([other, mine])))
        ff_got = across(ff_halves[0], 1), across(ff_halves[1], 2)
        ff_owned = []
        for bit, mine, other in zip(bits, ff_halves, ff_got):
            mine, other = mine.astype(F32), other.astype(F32)
            ff_owned.append((jnp.where(bit == 0, mine, other), jnp.where(bit == 0, other, mine)))
        grad_token_parts = after(grad_token_parts, parts)
        one = z_sum(parts[0], after(got, grad_token_parts))
        grad_token_parts = after(grad_token_parts, one)
        quarters = by_quarters(one, [across(one, step) for step in (1, 2, 3)])
        vectors = [i[:, wide + third :] for i in quarters]
        vectors = vectors[0] + vectors[1] + vectors[2] + vectors[3]
        joined = [jnp.concatenate(quarters[:2]), jnp.concatenate(quarters[2:])]
        owned_out = jnp.concatenate([one[:, wide : wide + third] for one in joined], 1)
        low, high = to_shard(*[one[:, :wide] for one in joined])
        owned_qkv = [i[:, kind * part : (kind + 1) * part] for kind in range(3) for i in (low, high)]
        owned_qkv = jnp.concatenate(owned_qkv, 1)
        half = local // 2
        blocks_in = [
            jnp.concatenate([jnp.concatenate([cut[:half], cut[half : 2 * half]], 1) for cut in one]) for one in ff_owned
        ]
        owned_in = jnp.concatenate(to_shard(*blocks_in), 1)
        owned_back = jnp.concatenate([cut[2 * half :] for one in ff_owned for cut in one])
    else:
        owned_back, owned_in = scatter_lines(grad_back), scatter_columns(grad_in).reshape(local, hidden)
        owned_out, owned_qkv = scatter_lines(grad_out), scatter_columns(grad_weight)
        owned_qkv = owned_qkv.reshape(local, ranks, groups, 3, lanes)
        owned_qkv = owned_qkv.transpose(0, 3, 1, 2, 4).reshape(local, 3 * width)

    if paired:
        total = (vectors + swap(vectors)).reshape(-1)
        sums, ff_sums_of = total[: 8 * width].reshape(8, width), total[8 * width : 8 * width + hidden]
    else:
        sums, ff_sums_of = lax.psum((sums, ff_sums_of), EVERY)
    grad_tokens = from_rows(*grad_token_parts)
    at = shard * spans + ctx
    mine = lax.dynamic_slice_in_dim(sums, at * (width // blocks), width // blocks, 1)
    ff_mine = lax.dynamic_slice_in_dim(ff_sums_of, at * (hidden // blocks), hidden // blocks, 0)
    return (
        output,
        grad_tokens,
        owned_qkv,
        owned_out,
        owned_in,
        owned_back,
        mine[0:2],
        mine[2:4],
        mine[4:8],
        ff_mine,
    )


def solution(mesh):
    rows = P(("replica", "shard"), "ctx", None)
    lines, columns, flat = P(LINE, None), P(None, LINE), P(LINE)
    return jax.shard_map(
        body,
        mesh=mesh,
        in_specs=(rows, lines, lines, lines, lines, columns, columns, columns, flat, rows),
        out_specs=(rows, rows, lines, lines, lines, lines, columns, columns, columns, flat),
        check_vma=False,
    )
```
